32 devices in a mesh: col: 8 (over z, core), sec: 4 (over y, x).
Axes of the slice: x: 2, y: 2, z: 4, core: 2. Of those that a mesh axis runs over, the one named last changes fastest.
Arguments:
- env_right: bfloat16 [1, 16384, 128], P(None, 'sec'), may hold values from -6 to 6
- transfer: bfloat16 [8, 1, 16384, 4, 128], P('col', None, 'sec'), may hold values from -0.25 to 0.25
- sources: int32 [8, 1, 128, 4], P('col', None, 'sec'), may hold values from 0 to 127, as said below
- env_left: bfloat16 [8, 1, 16384, 128], P('col', None, 'sec'), may hold values from -0.5 to 0.5
Outputs:
- env_out: bfloat16 [8, 1, 16384, 128], P('col', None, 'sec')
- grad: bfloat16 [8, 1, 16384, 4, 128], P('col', None, 'sec')
The draws below stay inside these ranges and needn't reach their ends.
Inputs may be any that keep to these rules, and one draw needn't show every extreme that they name: `sources`: every source tile lies within 2 tiles of its output tile; each list holds the tiles at offsets -2 and +2 (reflected at the ends of the space) and two of the offsets -1, 0, 1.
All inputs are finite; a program needn't handle non-finite values.
Results may differ from the reference program's by a relative error of at most 0.029.
Values may be sent and summed in bfloat16 or wider, within the bound.
No kernel may reach another device: no remote copies, remote signals or barrier semaphores. Data moves between devices by JAX's collectives and lax.ppermute only.
A program may use at most 64 MiB of HBM per device.

```python
import jax
import jax.numpy as jnp

K = 128
TILE = 128
PAIRS = 4
REACH = 2
ROWS = 1
NCOLS = 8
NT = 128
F = 16384


def draw_sources(key, part):
    dropped = jax.random.randint(key, (NCOLS, ROWS, NT), 0, 3)
    below = jnp.where(dropped == 0, 0, -1).astype(jnp.int32)
    above = jnp.where(dropped == 2, 0, 1).astype(jnp.int32)
    distant = jnp.full((NCOLS, ROWS, NT), REACH, jnp.int32)
    offsets = jnp.stack([-distant, distant, below, above], axis=-1)
    tile_index = jnp.arange(NT, dtype=jnp.int32)[None, None, :, None]
    source_tile = tile_index + offsets
    source_tile = jnp.where(source_tile < 0, -source_tile, source_tile)
    source_tile = jnp.where(source_tile > NT - 1, 2 * (NT - 1) - source_tile, source_tile)
    return source_tile.astype(jnp.int32)


def shard_levels(rng, dims, pieces, low, largest):
    factor_of = 1.0
    for dim, blocks in pieces:
        heights = jax.random.uniform(jax.random.fold_in(jax.random.fold_in(rng, 6), dim), (blocks,), jnp.float32, low / len(pieces), largest / len(pieces))
        factor_of = factor_of * jnp.repeat(jnp.exp(heights), dims[dim] // blocks).reshape((-1,) + (1,) * (len(dims) - 1 - dim))
    return factor_of


def gaussian(key, extent, spread, bound, cuts=(), kind=jnp.bfloat16):
    result = jax.random.normal(key, extent, jnp.float32) * spread
    if len(cuts) > 0:
        result = shard_levels(key, extent, cuts, -0.22, 0.18) * result
    return jnp.clip(result, min=-bound, max=bound).astype(kind)


def setup_inputs(seed: int = 0) -> dict:
    arg_keys = jax.random.split(jax.random.key(seed), 5)
    return {
        "env_right": gaussian(arg_keys[0], (ROWS, F, K), 1.0, 6.0, ((1, 4),)),
        "transfer": gaussian(arg_keys[1], (NCOLS, ROWS, F, PAIRS, TILE), (PAIRS * TILE) ** -0.5, 0.25, ((0, 8), (2, 4))),
        "sources": draw_sources(jax.random.fold_in(arg_keys[4], 71), 0),
        "env_left": gaussian(arg_keys[3], (NCOLS, ROWS, F, K), K ** -0.5, 0.5, ((0, 8), (2, 4))),
    }


def pick_blocks(state, source_list):
    blocks = state.reshape(ROWS, NT, TILE, K)

    def one_row(row_blocks, row_sources):
        return row_blocks[row_sources]

    return jax.vmap(one_row)(blocks, source_list)


def reference(env_right, transfer, sources, env_left):
    state = env_right
    env_list = []
    grad_list = []
    for column in reversed(range(NCOLS)):
        picked = pick_blocks(state, sources[column]).astype(jnp.float32)
        blocks = transfer[column].reshape(ROWS, NT, TILE, PAIRS, TILE).astype(jnp.float32)
        fresh = jnp.einsum('rtopq,rtpqk->rtok', blocks, picked)
        fresh = fresh.reshape(ROWS, F, K).astype(jnp.bfloat16)
        left = env_left[column].reshape(ROWS, NT, TILE, K).astype(jnp.float32)
        block_grad = jnp.einsum('rtok,rtpqk->rtopq', left, picked)
        grad_list.append(block_grad.reshape(ROWS, F, PAIRS, TILE).astype(jnp.bfloat16))
        env_list.append(fresh)
        state = fresh
    env_out = jnp.stack(env_list[::-1], axis=0)
    grad = jnp.stack(grad_list[::-1], axis=0)
    return env_out, grad
```

```python
import jax
import jax.numpy as jnp
from jax import lax
from jax.experimental import pallas as pl
from jax.experimental.pallas import tpu as pltpu
from jax.sharding import PartitionSpec as P

TILE = 128
REACH = 2
WIDE = 2 * REACH
GROUP = 4
VMEM = pl.BlockSpec(memory_space=pltpu.VMEM)
SMEM = pl.BlockSpec(memory_space=pltpu.SMEM)
ANY = pl.BlockSpec(memory_space=pl.ANY)


def params():
    return pltpu.CompilerParams(vmem_limit_bytes=24 * 1024 * 1024)


def rows_of(tile, count=1):
    start = tile * TILE
    if not isinstance(start, int):
        start = pl.multiple_of(start, TILE)
    return pl.ds(start, count * TILE)


def stacked(state, table, base, pairs):
    return jnp.concatenate([state[rows_of(table[base + j]), :] for j in range(pairs)], axis=0)


def product(blocks, state):
    return jnp.dot(blocks, state, preferred_element_type=jnp.float32).astype(jnp.bfloat16)


def flat(blocks, pairs):
    split = jnp.swapaxes(blocks, 0, 1)
    return jnp.concatenate([split[j] for j in range(pairs)], axis=1)


def prepare_own(tiles, extra, pairs, transfer):
    count = tiles // GROUP

    def kernel(source, packed, landed, arrived):
        copies = [
            pltpu.make_async_copy(source.at[rows_of(g * GROUP, GROUP)], landed.at[rows_of(g * GROUP, GROUP)], arrived.at[g])
            for g in range(count)
        ]
        for copy in copies:
            copy.start()
        for g in range(count):
            copies[g].wait()
            for i in range(g * GROUP, (g + 1) * GROUP):
                packed[rows_of(i), :] = flat(landed[rows_of(i)], pairs)

    return pl.pallas_call(
        kernel,
        in_specs=[ANY],
        out_specs=VMEM,
        out_shape=jax.ShapeDtypeStruct(((tiles + extra) * TILE, pairs * TILE), jnp.bfloat16),
        scratch_shapes=[pltpu.VMEM(transfer.shape, jnp.bfloat16), pltpu.SemaphoreType.DMA((count,))],
        compiler_params=params(),
        name="prepare_own",
    )(transfer)


def prepare_odd(tiles, pairs, ints, main, lower, upper, packed):
    count = tiles // GROUP

    def kernel(table, source, low, high, old, new, landed, arrived):
        @pl.when(table[2] == 1)
        def _():
            copies = [
                pltpu.make_async_copy(source.at[rows_of(g * GROUP, GROUP)], landed.at[rows_of(g * GROUP, GROUP)], arrived.at[g])
                for g in range(count)
            ]
            for copy in copies:
                copy.start()
            for i in range(REACH):
                new[rows_of(tiles + i), :] = flat(low[rows_of(i)], pairs)
                new[rows_of(2 * tiles + REACH + i), :] = flat(high[rows_of(i)], pairs)
            for g in range(count):
                copies[g].wait()
                for i in range(g * GROUP, (g + 1) * GROUP):
                    new[rows_of(tiles + REACH + i), :] = flat(landed[rows_of(i)], pairs)

    return pl.pallas_call(
        kernel,
        in_specs=[SMEM, ANY, VMEM, VMEM, VMEM],
        out_specs=VMEM,
        out_shape=jax.ShapeDtypeStruct(packed.shape, packed.dtype),
        input_output_aliases={4: 0},
        scratch_shapes=[pltpu.VMEM(main.shape, jnp.bfloat16), pltpu.SemaphoreType.DMA((count,))],
        compiler_params=params(),
        name="prepare_odd",
    )(ints, main, lower, upper, packed)


HEAD = 8


def own_step(kind, tiles, pairs, width, ints, main, lower, upper, packed, state=None):
    emit = width > 0

    def kernel(table, middle, low, high, blocks, *rest):
        kept = rest[0] if state is None else rest[1]
        outs = rest[1:] if state is None else rest[2:]

        @pl.when(table[3] == kind)
        def _():
            skip = low.shape[0] // TILE - REACH
            kept[rows_of(0, REACH), :] = low[rows_of(skip, REACH), :]
            kept[rows_of(REACH, tiles), :] = middle[...]
            kept[rows_of(REACH + tiles, REACH), :] = high[rows_of(0, REACH), :]
            if emit:
                advance_own(tiles, pairs, width, table, kept, blocks, *outs)

    return call_step(kernel, tiles, width, [ints, main, lower, upper, packed], state, main.shape[1], "own_step")


def advance_own(tiles, pairs, width, table, kept, blocks, out, first, last):
    for i in range(tiles):
        fresh = product(blocks[rows_of(i), :], stacked(kept, table, HEAD + pairs * i, pairs))
        out[rows_of(i), :] = fresh
        if i < width:
            first[rows_of(i), :] = fresh
        if i >= tiles - width:
            last[rows_of(i - (tiles - width)), :] = fresh


def call_step(kernel, tiles, width, operands, state, bond, name, scratch=()):
    def shape(count):
        return jax.ShapeDtypeStruct((count * TILE, bond), jnp.bfloat16)

    outs = [shape(tiles + 2 * REACH)]
    if width > 0:
        outs += [shape(tiles), shape(width), shape(width)]
    aliases = {}
    if state is not None:
        aliases = {len(operands): 0}
        operands = operands + [state]
    return pl.pallas_call(
        kernel,
        in_specs=[SMEM] + [VMEM] * (len(operands) - 1),
        out_specs=[VMEM] * len(outs),
        out_shape=outs,
        input_output_aliases=aliases,
        scratch_shapes=list(scratch),
        compiler_params=params(),
        name=name,
    )(*operands)


def pair_step(kind, tiles, pairs, width, ints, main, lower, upper, packed, state):
    odd = HEAD + pairs * tiles

    def kernel(table, middle, low, high, blocks, old, kept, *rest):
        outs, wide = rest[:-1], rest[-1]

        @pl.when(table[3] == kind)
        def _():
            wide[rows_of(0, WIDE), :] = low[...]
            wide[rows_of(WIDE, tiles), :] = middle[...]
            wide[rows_of(WIDE + tiles, WIDE), :] = high[...]
            for i in range(tiles + 2 * REACH):
                kept[rows_of(i), :] = product(blocks[rows_of(tiles + i), :], stacked(wide, table, odd + pairs * i, pairs))
            if width > 0:
                advance_own(tiles, pairs, width, table, kept, blocks, *outs)

    scratch = [pltpu.VMEM(((tiles + 2 * WIDE) * TILE, main.shape[1]), jnp.bfloat16)]
    return call_step(kernel, tiles, width, [ints, main, lower, upper, packed], state, main.shape[1], "pair_step", scratch)


def finish(tiles, pairs, ints, state, packed, left):
    bond = state.shape[1]
    count = tiles // GROUP

    def kernel(table, kept, blocks, rows, env, grad, staged, sent):
        copies = []
        for i in range(tiles):
            sources = stacked(kept, table, HEAD + pairs * i, pairs)
            env[rows_of(i), :] = product(blocks[rows_of(i), :], sources)
            block = lax.dot_general(rows[rows_of(i), :], sources, (((1,), (1,)), ((), ())), preferred_element_type=jnp.float32)
            block = block.astype(jnp.bfloat16)
            block = jnp.stack([block[:, j * TILE : (j + 1) * TILE] for j in range(pairs)], axis=0)
            staged[rows_of(i)] = jnp.swapaxes(block, 0, 1)
            if i % GROUP == GROUP - 1:
                span = rows_of(i + 1 - GROUP, GROUP)
                copies.append(pltpu.make_async_copy(staged.at[span], grad.at[span], sent.at[i // GROUP]))
                copies[-1].start()
        for copy in copies:
            copy.wait()

    return pl.pallas_call(
        kernel,
        in_specs=[SMEM, VMEM, VMEM, VMEM],
        out_specs=[VMEM, ANY],
        out_shape=[
            jax.ShapeDtypeStruct((tiles * TILE, bond), jnp.bfloat16),
            jax.ShapeDtypeStruct((tiles * TILE, pairs, TILE), jnp.bfloat16),
        ],
        scratch_shapes=[pltpu.VMEM((tiles * TILE, pairs, TILE), jnp.bfloat16), pltpu.SemaphoreType.DMA((count,))],
        compiler_params=params(),
        name="finish",
    )(ints, state, packed, left)


def per_device(env_right, transfer, sources, env_left):
    ncol, nsec = lax.axis_size("col"), lax.axis_size("sec")
    layers = ncol // 2
    col, sec = lax.axis_index("col"), lax.axis_index("sec")
    layer, core = col // 2, col % 2
    blocks = transfer[0, 0]
    length, pairs = blocks.shape[0], blocks.shape[1]
    tiles = length // TILE
    right, left = env_right[0], env_left[0, 0]

    def move(value, hops):
        both = [
            (a * nsec + s, b * nsec + s + by) for a, b, by in hops for s in range(nsec) if 0 <= s + by < nsec
        ]
        return lax.ppermute(value, ("col", "sec"), both)

    top = ncol - 1
    packed = prepare_own(tiles, tiles + 2 * REACH, pairs, blocks)

    lower = move(right[-REACH * TILE :], [(top - 1, top, 1)])
    upper = move(right[: REACH * TILE], [(top - 1, top, -1)])

    odd = [(2 * z + 1, 2 * z, 0) for z in range(layers - 1)]
    odd_main = move(blocks, odd)
    odd_sources = move(sources[0, 0], odd)

    def edge(block_rows, source_rows):
        coded = (source_rows - sec * tiles).astype(jnp.bfloat16)
        coded = jnp.broadcast_to(coded[:, :, None], (REACH, pairs, TILE))
        return jnp.concatenate([block_rows, coded], axis=0)

    low_edge = move(edge(blocks[-REACH * TILE :], sources[0, 0, -REACH:]), [(a, b, 1) for a, b, _ in odd])
    high_edge = move(edge(blocks[: REACH * TILE], sources[0, 0, :REACH]), [(a, b, -1) for a, b, _ in odd])
    low_sources = low_edge[REACH * TILE :, :, 0].astype(jnp.int32) - tiles
    high_sources = high_edge[REACH * TILE :, :, 0].astype(jnp.int32) + tiles

    own_local = jnp.clip(sources[0, 0] - sec * tiles + REACH, 0, tiles + 2 * REACH - 1)
    odd_local = jnp.concatenate([low_sources, odd_sources - sec * tiles, high_sources], axis=0)
    odd_local = jnp.clip(odd_local + WIDE, 0, tiles + 2 * WIDE - 1)

    kind = 2 * (layers - 1 - layer) + core
    takes_odd = jnp.logical_and(core == 0, layer < layers - 1).astype(jnp.int32)
    zero = jnp.zeros((), jnp.int32)
    head = jnp.stack([col, sec, takes_odd, kind, zero, zero, zero, zero]).astype(jnp.int32)
    own_ints = jnp.concatenate([head, own_local.reshape(-1)])
    ints = jnp.concatenate([own_ints, odd_local.reshape(-1)])

    state, main, first, last = own_step(1, tiles, pairs, REACH, own_ints, right, lower, upper, packed)
    lower = move(last, [(top, top - 1, 1)])
    upper = move(first, [(top, top - 1, -1)])
    main = move(main, [(c, c ^ 1, 0) for c in range(ncol)])
    state, main, first, last = own_step(0, tiles, pairs, WIDE, own_ints, main, lower, upper, packed, state)
    packed = prepare_odd(tiles, pairs, ints, odd_main, low_edge[: REACH * TILE], high_edge[: REACH * TILE], packed)

    for step in range(1, layers):
        above, here = 2 * (layers - step), 2 * (layers - 1 - step)
        main = move(main, [(above, here, 0)])
        lower = move(last, [(above, here, 1)])
        upper = move(first, [(above, here, -1)])
        passed = [move(value, [(c, c ^ 1, 0) for c in range(ncol)]) for value in (main, lower, upper)]
        if step < layers - 1:
            state, main, first, last = pair_step(2 * step, tiles, pairs, WIDE, ints, main, lower, upper, packed, state)
        else:
            (state,) = pair_step(2 * step, tiles, pairs, 0, ints, main, lower, upper, packed, state)
        (state,) = own_step(2 * step + 1, tiles, pairs, 0, own_ints, *passed, packed, state)

    env, grad = finish(tiles, pairs, own_ints, state, packed, left)
    return env[None, None], grad[None, None]


def solution(mesh):
    placed = (
        P(None, "sec", None),
        P("col", None, "sec", None, None),
        P("col", None, "sec", None),
        P("col", None, "sec", None),
    )
    return jax.shard_map(
        per_device,
        mesh=mesh,
        in_specs=placed,
        out_specs=(P("col", None, "sec", None), P("col", None, "sec", None, None)),
        check_vma=False,
    )
```

```python
import jax
import jax.numpy as jnp
from jax import lax
from jax.experimental import pallas as pl
from jax.experimental.pallas import tpu as pltpu
from jax.sharding import PartitionSpec as P

TILE = 128
REACH = 2
WIDE = 2 * REACH
BAND = 2 * REACH + 1
GROUP = 4
VMEM = pl.BlockSpec(memory_space=pltpu.VMEM)
SMEM = pl.BlockSpec(memory_space=pltpu.SMEM)
HBM = pl.BlockSpec(memory_space=pltpu.HBM)


def params():
    return pltpu.CompilerParams(vmem_limit_bytes=16 * 1024 * 1024)


def cost(flops):
    return pl.CostEstimate(flops=int(flops), bytes_accessed=0, transcendentals=0)


def rows_of(tile, count=1):
    start = tile * TILE
    if not isinstance(start, int):
        start = pl.multiple_of(start, TILE)
    return pl.ds(start, count * TILE)


def tile_rows(count, width):
    return jax.ShapeDtypeStruct((count * TILE, width), jnp.bfloat16)


def kind_here():
    ncol, col = lax.axis_size("col"), lax.axis_index("col")
    return 2 * (ncol // 2 - 1 - col // 2) + col % 2


def reversed_here():
    return lax.axis_index("sec") % 2 == 0


def partner(s):
    return s + 1 if s % 2 == 0 else s - 1


def other(s):
    return s - 1 if s % 2 == 0 else s + 1


def places(table, tiles):
    back = reversed_here()
    base = lax.axis_index("sec") * tiles
    sign, flip = jnp.where(back, -1, 1), jnp.where(back, tiles - 1, 0)
    origin = jnp.where(back, tiles - 1 + base, -base)
    return lambda j, p: sign * table[j, sign * p + flip] + origin


def stacked(state, place, p, shift, pairs):
    return jnp.concatenate([state[rows_of(place(j, p) + shift), :] for j in range(pairs)], axis=0)


def product(blocks, state):
    return jnp.dot(blocks, state, preferred_element_type=jnp.float32).astype(jnp.bfloat16)


def blocks_at(parts, cuts, p):
    k = max(k for k in range(len(cuts) - 1) if cuts[k] <= p)
    return parts[k][rows_of(p - cuts[k]), :]


def prepare(cuts, k, pairs, tiles, table, transfer):
    begin, end = cuts[k], cuts[k + 1]
    groups = [(p, min(GROUP, end - p)) for p in range(begin, end, GROUP)]
    edges = [range(REACH)] * (k == 0) + [range(tiles - REACH, tiles)] * (end == tiles)

    def kernel(table, source, packed, *rest):
        *edge_refs, landed, arrived = rest
        back = reversed_here()
        place = places(table, tiles)
        copies = []
        for g, (p, size) in enumerate(groups):
            start = jnp.where(back, tiles - p - size, p)
            copies.append(pltpu.make_async_copy(source.at[rows_of(start, size)], landed.at[rows_of(p - begin, size)], arrived.at[g]))
            copies[-1].start()
        for edge in edge_refs:
            edge[...] = jnp.zeros_like(edge)
        for g, (p, size) in enumerate(groups):
            copies[g].wait()
            for i in range(size):
                at = p - begin + jnp.where(back, size - 1 - i, i)
                split = jnp.swapaxes(landed[rows_of(at)], 0, 1)
                for j in range(pairs):
                    packed[rows_of(p + i - begin), j * TILE : (j + 1) * TILE] = split[j]
                for edge, span in zip(edge_refs, edges):
                    if p + i in span:
                        for j in range(pairs):
                            edge[rows_of(span.index(p + i)), rows_of(REACH - place(j, p + i) + p + i)] = split[j]

    size = end - begin
    return pl.pallas_call(
        kernel,
        in_specs=[SMEM, HBM],
        out_specs=[VMEM] * (1 + len(edges)),
        out_shape=[tile_rows(size, pairs * TILE)] + [tile_rows(REACH, BAND * TILE)] * len(edges),
        scratch_shapes=[pltpu.VMEM((size * TILE, pairs, TILE), jnp.bfloat16), pltpu.SemaphoreType.DMA((len(groups),))],
        compiler_params=params(),
        cost_estimate=cost(1e11 * size / tiles),
        name="prepare",
    )(table, pltpu.with_memory_space_constraint(transfer, pltpu.HBM))


def pair_step(step, k, tiles, pairs, cuts, inner, outer, tables, own, odd, edges, arrived, keeps):
    count = len(own)
    head, tail = k == 0, k == count - 1
    edges = edges[:1] * head + edges[1:] * tail
    bond = keeps[0].shape[1] if keeps else arrived[0].shape[1]
    begin, end = inner[k], inner[k + 1]
    emit = outer is not None
    out = (outer[k], outer[k + 1]) if emit else None
    begin_odd, end_odd = 0 if head else begin - REACH, tiles if tail else end - REACH
    odd_parts = [i for i in range(count) if cuts[i] < end_odd and cuts[i + 1] > begin_odd]
    own_parts = [i for i in range(count) if emit and cuts[i] < out[1] and cuts[i + 1] > out[0]]
    fixed = [*(own[i] for i in own_parts), *(odd[i] for i in odd_parts), *edges]
    first = 2 + len(fixed) + len(arrived)

    def kernel(table, odd_table, *refs):
        own_refs = dict(zip(own_parts, refs))
        odd_refs = dict(zip(odd_parts, refs[len(own_parts) :]))
        edge_refs = refs[len(own_parts) + len(odd_parts) : len(fixed)]
        came = refs[len(fixed) : first - 2]
        kept, wide, *outs = refs[first - 2 + len(keeps) :]
        kind = kind_here()
        place, odd_place = places(table, tiles), places(odd_table, tiles)

        def take_first():
            low, right, high = came
            back = reversed_here()
            for m in range(WIDE):
                wide[rows_of(jnp.where(back, tiles + 2 * WIDE - 1 - m, m)), :] = low[rows_of(m), :]
                wide[rows_of(jnp.where(back, WIDE - 1 - m, tiles + WIDE + m)), :] = high[rows_of(m), :]
            for p in range(tiles):
                wide[rows_of(WIDE + p), :] = right[rows_of(jnp.where(back, tiles - 1 - p, p)), :]

        @pl.when(kind == 2 * step)
        def _():
            if step > 0:
                wide[rows_of(WIDE + begin, end - begin), :] = came[0][...]
                for m in range(WIDE):
                    if head:
                        wide[rows_of(WIDE - 1 - m), :] = came[1][rows_of(m), :]
                    if tail:
                        wide[rows_of(tiles + 2 * WIDE - 1 - m), :] = came[-1][rows_of(m), :]
            elif head:
                take_first()
            for e in range(REACH):
                if head:
                    kept[rows_of(REACH - 1 - e), :] = product(edge_refs[0][rows_of(e), :], wide[rows_of(WIDE - 1 - e - REACH, BAND), :])
                if tail:
                    at = tiles + REACH - 1 - e
                    kept[rows_of(REACH + at), :] = product(edge_refs[-1][rows_of(e), :], wide[rows_of(WIDE + at - REACH, BAND), :])
            for p in range(begin_odd, end_odd):
                kept[rows_of(REACH + p), :] = product(blocks_at(odd_refs, cuts, p), stacked(wide, odd_place, p, WIDE, pairs))
            for p in range(*(out or (0, 0))):
                fresh = product(blocks_at(own_refs, cuts, p), stacked(kept, place, p, REACH, pairs))
                outs[0][rows_of(p - out[0]), :] = fresh
                if p < WIDE:
                    outs[1][rows_of(p), :] = fresh
                if p >= tiles - WIDE:
                    outs[-1][rows_of(p - (tiles - WIDE)), :] = fresh

        if step == 0 and head:

            @pl.when(kind == 1)
            def _():
                take_first()
                kept[...] = wide[rows_of(REACH, tiles + 2 * REACH), :]

    outs = [tile_rows(tiles + 2 * REACH, bond), tile_rows(tiles + 2 * WIDE, bond)]
    if emit:
        outs += [tile_rows(out[1] - out[0], bond)] + [tile_rows(WIDE, bond)] * (head + tail)
    return pl.pallas_call(
        kernel,
        in_specs=[SMEM] * 2 + [VMEM] * (first - 2 + len(keeps)),
        out_specs=[VMEM] * len(outs),
        out_shape=outs,
        input_output_aliases={first + i: i for i in range(len(keeps))},
        compiler_params=params(),
        cost_estimate=cost(1e10 * (end - begin) / tiles),
        name="pair_step",
    )(*tables, *fixed, *arrived, *keeps)


def finish(tiles, pairs, cuts, table, own, given, left, state):
    bond = state.shape[1]
    count = len(own)
    groups = [(p, GROUP) for p in range(0, tiles, GROUP)]

    def kernel(table, *refs):
        own_refs = refs[:count]
        given, rows, old, kept, env, grad, staged, sent = refs[count:]
        kind = kind_here()

        @pl.when((kind % 2 == 1) & (kind > 1))
        def _():
            kept[...] = given[rows_of(REACH, tiles + 2 * REACH), :]

        place = places(table, tiles)
        back = reversed_here()
        copies = []
        for g, (p, size) in enumerate(groups):
            start = jnp.where(back, tiles - p - size, p)
            for i in range(size):
                inside = jnp.where(back, size - 1 - i, i)
                sources = stacked(kept, place, p + i, REACH, pairs)
                env[rows_of(start + inside), :] = product(blocks_at(own_refs, cuts, p + i), sources)
                block = lax.dot_general(
                    rows[rows_of(start + inside), :], sources, (((1,), (1,)), ((), ())), preferred_element_type=jnp.float32
                ).astype(jnp.bfloat16)
                block = jnp.stack([block[:, j * TILE : (j + 1) * TILE] for j in range(pairs)], axis=0)
                staged[rows_of(p + inside)] = jnp.swapaxes(block, 0, 1)
            copies.append(pltpu.make_async_copy(staged.at[rows_of(p, size)], grad.at[rows_of(start, size)], sent.at[g]))
            copies[-1].start()
        for copy in copies:
            copy.wait()

    grad = jax.ShapeDtypeStruct((tiles * TILE, pairs, TILE), jnp.bfloat16)
    operands = [*own, given, left, state]
    _, env, grad = pl.pallas_call(
        kernel,
        in_specs=[SMEM] + [VMEM] * len(operands),
        out_specs=[VMEM, VMEM, HBM],
        out_shape=[tile_rows(tiles + 2 * REACH, bond), tile_rows(tiles, bond), grad],
        input_output_aliases={len(operands): 0},
        scratch_shapes=[pltpu.VMEM(grad.shape, jnp.bfloat16), pltpu.SemaphoreType.DMA((len(groups),))],
        compiler_params=params(),
        cost_estimate=cost(5e10),
        name="finish",
    )(table, *operands)
    return env, grad


def limits(tiles, crossings):
    room = WIDE * crossings
    ends = [e for e in (3 * tiles // 8, 3 * tiles // 4) if room <= e <= tiles - WIDE]
    return ends or ([tiles - WIDE] if room <= tiles - WIDE else [])


def per_device(env_right, transfer, sources, env_left):
    ncol, nsec = lax.axis_size("col"), lax.axis_size("sec")
    layers = ncol // 2
    blocks = transfer[0, 0]
    length, pairs = blocks.shape[0], blocks.shape[1]
    tiles = length // TILE
    right, left = env_right[0], env_left[0, 0]

    def move(value, hops):
        both = [(a * nsec + s, b * nsec + to(s)) for a, b, to in hops for s in range(nsec) if 0 <= to(s) < nsec]
        return lax.ppermute(value, ("col", "sec"), both)

    def same(s):
        return s

    swap = [(c, c ^ 1, same) for c in range(ncol)]
    top = ncol - 1

    low = move(right[-WIDE * TILE :], [(c - 2, c, lambda s: s + 1) for c in (top - 1, top)])
    high = move(right[: WIDE * TILE], [(c - 2, c, lambda s: s - 1) for c in (top - 1, top)])

    table = sources[0, 0].T

    ends = limits(tiles, layers - 1)
    count = len(ends) + 1
    cuts = [0] + [e + WIDE - REACH for e in ends] + [tiles]
    own, edges = [], []
    for k in range(count):
        part, *edge = prepare(cuts, k, pairs, tiles, table, blocks)
        own.append(part)
        edges += edge
    odd_cols = [(2 * z + 1, 2 * z) for z in range(layers)]
    odd = [move(part, [(a, b, same) for a, b in odd_cols]) for part in own]
    odd_table = move(table, [(a, b, same) for a, b in odd_cols])
    odd_edges = [move(edges[0], [(a, b, partner) for a, b in odd_cols]), move(edges[1], [(a, b, other) for a, b in odd_cols])]

    keeps = []
    sent = None
    for step in range(layers):
        end = step == layers - 1
        inner = [0] + [e - WIDE * (step - 1) for e in ends] + [tiles]
        outer = None if end else [0] + [e - WIDE * step for e in ends] + [tiles]
        above, here = 2 * (layers - step), 2 * (layers - 1 - step)
        leaving = []
        for k in range(count):
            if step == 0:
                came = [low, right, high] if k == 0 else []
            else:
                came = [move(sent[k][0], [(above, here, same)])]
                tail = sent[k][1:]
                if k == 0:
                    came.append(move(tail[0], [(above, here, partner)]))
                if k == count - 1:
                    came.append(move(tail[-1], [(above, here, other)]))
            result = pair_step(step, k, tiles, pairs, cuts, inner, outer, [table, odd_table], own, odd, odd_edges, came, keeps)
            keeps = result[:2]
            leaving.append(result[2:])
        sent = leaving

    given = move(keeps[1], swap)
    env, grad = finish(tiles, pairs, cuts, table, own, given, left, keeps[0])
    return env[None, None], grad[None, None]


def solution(mesh):
    placed = (
        P(None, "sec", None),
        P("col", None, "sec", None, None),
        P("col", None, "sec", None),
        P("col", None, "sec", None),
    )
    return jax.shard_map(
        per_device,
        mesh=mesh,
        in_specs=placed,
        out_specs=(P("col", None, "sec", None), P("col", None, "sec", None, None)),
        check_vma=False,
    )
```

```python
import jax
import jax.numpy as jnp
from jax import lax
from jax.experimental import pallas as pl
from jax.experimental.pallas import tpu as pltpu
from jax.sharding import PartitionSpec as P

TILE = 128
REACH = 2
WIDE = 2 * REACH
BAND = 2 * REACH + 1
GROUP = 4
PREPARE, FIRST, STEP, FINISH = 1e10, 2e10, 1e10, 4e9
VMEM = pl.BlockSpec(memory_space=pltpu.VMEM)
SMEM = pl.BlockSpec(memory_space=pltpu.SMEM)
HBM = pl.BlockSpec(memory_space=pltpu.HBM)


def params():
    return pltpu.CompilerParams(vmem_limit_bytes=16 * 1024 * 1024)


def cost(flops):
    return pl.CostEstimate(flops=int(flops), bytes_accessed=0, transcendentals=0)


def rows_of(tile, count=1):
    start = tile * TILE
    if not isinstance(start, int):
        start = pl.multiple_of(start, TILE)
    return pl.ds(start, count * TILE)


def tile_rows(count, width):
    return jax.ShapeDtypeStruct((count * TILE, width), jnp.bfloat16)


def kind_here():
    ncol, col = lax.axis_size("col"), lax.axis_index("col")
    return 2 * (ncol // 2 - 1 - col // 2) + col % 2


def reversed_here():
    return lax.axis_index("sec") % 2 == 0


def partner(s):
    return s + 1 if s % 2 == 0 else s - 1


def other(s):
    return s - 1 if s % 2 == 0 else s + 1


def places(table, tiles):
    back = reversed_here()
    base = lax.axis_index("sec") * tiles
    sign, flip = jnp.where(back, -1, 1), jnp.where(back, tiles - 1, 0)
    origin = jnp.where(back, tiles - 1 + base, -base)
    return lambda j, p: sign * table[j, sign * p + flip] + origin


def stacked(state, place, p, shift, pairs):
    return jnp.concatenate([state[rows_of(place(j, p) + shift), :] for j in range(pairs)], axis=0)


def product(blocks, state):
    return jnp.dot(blocks, state, preferred_element_type=jnp.float32).astype(jnp.bfloat16)


def blocks_at(parts, cuts, p):
    k = max(k for k in range(len(cuts) - 1) if cuts[k] <= p)
    return parts[k][rows_of(p - cuts[k]), :]


def prepare(first, final, cuts, pairs, table, transfer, right):
    tiles, bond = cuts[-1], right.shape[1]
    chosen = range(first, final)
    groups = [(p, min(GROUP, cuts[k + 1] - p)) for k in chosen for p in range(cuts[k], cuts[k + 1], GROUP)]
    begin, end = cuts[first], cuts[final]
    head, tail = first == 0, end == tiles
    spans = [range(WIDE)] * head + [range(tiles - WIDE, tiles)] * tail

    def kernel(table, source, environment, *refs):
        parts, refs = refs[: len(chosen)], refs[len(chosen) :]
        edges, refs = refs[: len(spans)], refs[len(spans) :]
        landed, halo, arrived, halo_arrived, placed = refs[-5:]
        back = reversed_here()
        place = places(table, tiles)
        copies, halos, whole = [], [], []
        for g, (p, size) in enumerate(groups):
            start = jnp.where(back, tiles - p - size, p)
            copies.append(pltpu.make_async_copy(source.at[rows_of(start, size)], landed.at[rows_of(p - begin, size)], arrived.at[g]))
        for e, span in enumerate(spans):
            start = jnp.where(back, tiles - span[0] - WIDE, span[0])
            halos.append(pltpu.make_async_copy(environment.at[rows_of(start, WIDE)], halo.at[e], halo_arrived.at[e]))
        if tail:
            for p in range(tiles):
                at = jnp.where(back, tiles - 1 - p, p)
                whole.append(pltpu.make_async_copy(environment.at[rows_of(at)], refs[0].at[rows_of(WIDE + p)], placed.at[p]))
        for copy in copies + halos + whole:
            copy.start()
        for edge in edges:
            edge[...] = jnp.zeros_like(edge)
        for g, (p, size) in enumerate(groups):
            copies[g].wait()
            k = max(k for k in chosen if cuts[k] <= p)
            for i in range(size):
                at = p - begin + jnp.where(back, size - 1 - i, i)
                split = jnp.swapaxes(landed[rows_of(at)], 0, 1)
                for j in range(pairs):
                    parts[k - first][rows_of(p + i - cuts[k]), j * TILE : (j + 1) * TILE] = split[j]
                for edge, span in zip(edges, spans):
                    near = span[:REACH] if span[0] == 0 else span[REACH:]
                    if p + i in near:
                        for j in range(pairs):
                            edge[rows_of(near.index(p + i)), rows_of(REACH - place(j, p + i) + p + i)] = split[j]
        for e, edge in enumerate(edges):
            halos[e].wait()
            for m in range(WIDE):
                at = jnp.where(back, WIDE - 1 - m, m)
                edge[rows_of(REACH), m * bond : (m + 1) * bond] = halo[e, rows_of(at), :]
        for copy in whole:
            copy.wait()

    outs = [tile_rows(cuts[k + 1] - cuts[k], pairs * TILE) for k in chosen] + [tile_rows(REACH + 1, BAND * TILE)] * len(spans)
    if tail:
        outs.append(tile_rows(tiles + 2 * WIDE, bond))
    return pl.pallas_call(
        kernel,
        in_specs=[SMEM, HBM, HBM],
        out_specs=[VMEM] * len(outs),
        out_shape=outs,
        scratch_shapes=[
            pltpu.VMEM(((end - begin) * TILE, pairs, TILE), jnp.bfloat16),
            pltpu.VMEM((len(spans), WIDE * TILE, bond), jnp.bfloat16),
            pltpu.SemaphoreType.DMA((len(groups),)),
            pltpu.SemaphoreType.DMA((len(spans),)),
            pltpu.SemaphoreType.DMA((tiles,)),
        ],
        compiler_params=params(),
        cost_estimate=cost(PREPARE * (end - begin) / tiles),
        name="prepare",
    )(table, *(pltpu.with_memory_space_constraint(value, pltpu.HBM) for value in (transfer, right)))


def pair_step(step, k, tiles, pairs, cuts, inner, outer, tables, own, odd, edges, arrived, keeps, give=()):
    count = len(own)
    head, tail = k == 0, k == count - 1
    edges = edges[:1] * head + edges[1:] * tail
    bond = keeps[-1].shape[1]
    begin, end = inner[k], inner[k + 1]
    emit = outer is not None
    out = (outer[k], outer[k + 1]) if emit else None
    begin_odd, end_odd = 0 if head else begin - REACH, tiles if tail else end - REACH
    odd_parts = [i for i in range(count) if cuts[i] < end_odd and cuts[i + 1] > begin_odd]
    own_parts = [i for i in range(count) if emit and cuts[i] < out[1] and cuts[i + 1] > out[0]]
    fixed = [*(own[i] for i in own_parts), *(odd[i] for i in odd_parts), *edges]
    first = 2 + len(fixed) + len(arrived)

    def kernel(table, odd_table, *refs):
        own_refs = dict(zip(own_parts, refs))
        odd_refs = dict(zip(odd_parts, refs[len(own_parts) :]))
        edge_refs = refs[len(own_parts) + len(odd_parts) : len(fixed)]
        came = refs[len(fixed) : first - 2]
        kept, wide, *outs = refs[first - 2 + len(keeps) :]
        kind = kind_here()
        place, odd_place = places(table, tiles), places(odd_table, tiles)

        @pl.when(kind == 2 * step)
        def _():
            if step > 0:
                wide[rows_of(WIDE + begin, end - begin), :] = came[0][...]
            for m in range(WIDE):
                if head:
                    value = came[1][rows_of(m), :] if step > 0 else edge_refs[0][rows_of(REACH), m * bond : (m + 1) * bond]
                    wide[rows_of(WIDE - 1 - m), :] = value
                if tail:
                    value = came[-1][rows_of(m), :] if step > 0 else edge_refs[-1][rows_of(REACH), m * bond : (m + 1) * bond]
                    wide[rows_of(tiles + 2 * WIDE - 1 - m), :] = value
            for e in range(REACH):
                if head:
                    kept[rows_of(REACH - 1 - e), :] = product(edge_refs[0][rows_of(e), :], wide[rows_of(WIDE - 1 - e - REACH, BAND), :])
                if tail:
                    at = tiles + REACH - 1 - e
                    kept[rows_of(REACH + at), :] = product(edge_refs[-1][rows_of(e), :], wide[rows_of(WIDE + at - REACH, BAND), :])
            for p in range(begin_odd, end_odd):
                kept[rows_of(REACH + p), :] = product(blocks_at(odd_refs, cuts, p), stacked(wide, odd_place, p, WIDE, pairs))
            for p in range(*(out or (0, 0))):
                fresh = product(blocks_at(own_refs, cuts, p), stacked(kept, place, p, REACH, pairs))
                outs[0][rows_of(p - out[0]), :] = fresh
                if p < WIDE:
                    outs[1][rows_of(p), :] = fresh
                if p >= tiles - WIDE:
                    outs[-1][rows_of(p - (tiles - WIDE)), :] = fresh

        if give:

            @pl.when(kind % 2 == 0)
            def _():
                for (low, high), out in zip(give, outs[len(outs) - len(give) :]):
                    out[...] = wide[rows_of(WIDE + low, high - low), :]

    outs = [tile_rows(tiles + 2 * REACH, bond), tile_rows(tiles + 2 * WIDE, bond)]
    if emit:
        outs += [tile_rows(out[1] - out[0], bond)] + [tile_rows(WIDE, bond)] * (head + tail)
    outs += [tile_rows(high - low, bond) for low, high in give]
    return pl.pallas_call(
        kernel,
        in_specs=[SMEM] * 2 + [VMEM] * (first - 2 + len(keeps)),
        out_specs=[VMEM] * len(outs),
        out_shape=outs,
        input_output_aliases={first + i: 2 - len(keeps) + i for i in range(len(keeps))},
        compiler_params=params(),
        cost_estimate=cost(STEP * (end - begin) / tiles if step or k else FIRST),
        name="pair_step",
    )(*tables, *fixed, *arrived, *keeps)


def finish(begin, end, tiles, pairs, cuts, table, own, given, regions, left, state, done):
    bond = state.shape[1]
    parts = [k for k in range(len(own)) if cuts[k] < end and cuts[k + 1] > begin]
    groups = [(p, min(GROUP, end - p)) for p in range(begin, end, GROUP)]
    refs_in = [*(own[k] for k in parts), *given, left, state, *done]
    count, fixed = len(parts), len(parts) + len(given) + 2

    def kernel(table, *refs):
        own_refs = dict(zip(parts, refs))
        *taken, rows = refs[count : fixed - 1]
        kept, env, grad, staged_env, staged, sent = refs[len(refs_in) :]

        @pl.when(kind_here() % 2 == 1)
        def _():
            for (low, high), value in zip(regions, taken):
                kept[rows_of(REACH + low, high - low), :] = value[...]

        place = places(table, tiles)
        back = reversed_here()
        copies = []
        for g, (p, size) in enumerate(groups):
            start = jnp.where(back, tiles - p - size, p)
            for i in range(size):
                inside = jnp.where(back, size - 1 - i, i)
                sources = stacked(kept, place, p + i, REACH, pairs)
                staged_env[rows_of(p - begin + inside), :] = product(blocks_at(own_refs, cuts, p + i), sources)
                block = lax.dot_general(
                    rows[rows_of(start + inside), :], sources, (((1,), (1,)), ((), ())), preferred_element_type=jnp.float32
                ).astype(jnp.bfloat16)
                block = jnp.stack([block[:, j * TILE : (j + 1) * TILE] for j in range(pairs)], axis=0)
                staged[rows_of(p - begin + inside)] = jnp.swapaxes(block, 0, 1)
            here, there = rows_of(p - begin, size), rows_of(start, size)
            copies.append(pltpu.make_async_copy(staged_env.at[here], env.at[there], sent.at[0, g]))
            copies.append(pltpu.make_async_copy(staged.at[here], grad.at[there], sent.at[1, g]))
            for copy in copies[-2:]:
                copy.start()
        for copy in copies:
            copy.wait()

    env = tile_rows(tiles, bond)
    grad = jax.ShapeDtypeStruct((tiles * TILE, pairs, TILE), jnp.bfloat16)
    size = (end - begin) * TILE
    return pl.pallas_call(
        kernel,
        in_specs=[SMEM] + [VMEM] * fixed + [HBM] * len(done),
        out_specs=[VMEM, HBM, HBM],
        out_shape=[tile_rows(tiles + 2 * REACH, bond), env, grad],
        input_output_aliases={fixed + i: i for i in range(1 + len(done))},
        scratch_shapes=[
            pltpu.VMEM((size, bond), jnp.bfloat16),
            pltpu.VMEM((size, pairs, TILE), jnp.bfloat16),
            pltpu.SemaphoreType.DMA((2, len(groups))),
        ],
        compiler_params=params(),
        cost_estimate=cost(FINISH * (end - begin) / tiles),
        name="finish",
    )(table, *refs_in)


def limits(tiles, crossings):
    room = WIDE * crossings
    ends = [e for e in (3 * tiles // 8, 3 * tiles // 4) if room <= e <= tiles - WIDE]
    return ends or [tiles - WIDE]


def per_device(env_right, transfer, sources, env_left):
    ncol, nsec = lax.axis_size("col"), lax.axis_size("sec")
    layers = ncol // 2
    blocks = transfer[0, 0]
    length, pairs = blocks.shape[0], blocks.shape[1]
    tiles = length // TILE
    right, left = env_right[0], env_left[0, 0]

    def move(value, hops):
        both = [(a * nsec + s, b * nsec + to(s)) for a, b, to in hops for s in range(nsec) if 0 <= to(s) < nsec]
        return lax.ppermute(value, ("col", "sec"), both)

    def same(s):
        return s

    swap = [(c, c ^ 1, same) for c in range(ncol)]

    table = sources[0, 0].T

    ends = limits(tiles, layers - 1)
    count = len(ends) + 1
    cuts = [0] + [e + WIDE - REACH for e in ends] + [tiles]
    head, first_edge = prepare(0, 1, cuts, pairs, table, blocks, right)
    *rest, last_edge, wide = prepare(1, count, cuts, pairs, table, blocks, right)
    own = [head, *rest]
    odd_cols = [(2 * z + 1, 2 * z) for z in range(layers)]
    odd = [move(part, swap) for part in own]
    odd_table = move(table, swap)
    odd_edges = [move(first_edge, [(a, b, partner) for a, b in odd_cols]), move(last_edge, [(a, b, other) for a, b in odd_cols])]

    keeps = [wide]
    sent = None
    for step in range(layers):
        end = step == layers - 1
        inner = [0] + [e - WIDE * (step - 1) for e in ends] + [tiles]
        outer = None if end else [0] + [e - WIDE * step for e in ends] + [tiles]
        above, here = 2 * (layers - step), 2 * (layers - 1 - step)
        leaving = []
        for k in range(count):
            came = []
            if step > 0:
                came = [move(sent[k][0], [(above, here, same)])]
                if k == 0:
                    came.append(move(sent[k][1], [(above, here, partner)]))
                if k == count - 1:
                    came.append(move(sent[k][-1], [(above, here, other)]))
            give = []
            if end and k == count - 2:
                middle = inner[k + 1] // 2
                give = [(-REACH, middle), (middle, inner[k + 1])]
            if end and k == count - 1:
                give = [(inner[k], tiles + REACH)]
            result = pair_step(step, k, tiles, pairs, cuts, inner, outer, [table, odd_table], own, odd, odd_edges, came, keeps, give)
            keeps = result[:2]
            if give:
                given = [move(value, swap) for value in result[len(result) - len(give) :]]
                if k == count - 2:
                    half = max(0, inner[k + 1] - WIDE) // GROUP * GROUP
                    state, *done = finish(0, half, tiles, pairs, cuts, table, own, given, give, left, keeps[0], [])
                    keeps = [state, keeps[1]]
                else:
                    _, env, grad = finish(half, tiles, tiles, pairs, cuts, table, own, given, give, left, keeps[0], done)
            leaving.append(result[2:])
        sent = leaving

    return env[None, None], grad[None, None]


def solution(mesh):
    placed = (
        P(None, "sec", None),
        P("col", None, "sec", None, None),
        P("col", None, "sec", None),
        P("col", None, "sec", None),
    )
    return jax.shard_map(
        per_device,
        mesh=mesh,
        in_specs=placed,
        out_specs=(P("col", None, "sec", None), P("col", None, "sec", None, None)),
        check_vma=False,
    )
```

```python
import jax
import jax.numpy as jnp
from jax import lax
from jax.experimental import pallas as pl
from jax.experimental.pallas import tpu as pltpu
from jax.sharding import PartitionSpec as P

TILE = 128
REACH = 2
WIDE = 2 * REACH
BAND = 2 * REACH + 1
GROUP = 4
FILL, EDGE, MAIN = range(3)
PREPARE, FIRST, SECOND, STEP, COLLECT, FINISH = 1e9, 2e10, 2e10, 1e10, 1e9, 4e9
VMEM = pl.BlockSpec(memory_space=pltpu.VMEM)
SMEM = pl.BlockSpec(memory_space=pltpu.SMEM)
HBM = pl.BlockSpec(memory_space=pltpu.HBM)


def params():
    return pltpu.CompilerParams(vmem_limit_bytes=16 * 1024 * 1024)


def cost(flops):
    return pl.CostEstimate(flops=int(flops), bytes_accessed=0, transcendentals=0)


def rows_of(tile, count=1):
    start = tile * TILE
    if not isinstance(start, int):
        start = pl.multiple_of(start, TILE)
    return pl.ds(start, count * TILE)


def tile_rows(count, width):
    return jax.ShapeDtypeStruct((count * TILE, width), jnp.bfloat16)


def kind_here():
    ncol, col = lax.axis_size("col"), lax.axis_index("col")
    return 2 * (ncol // 2 - 1 - col // 2) + col % 2


def reversed_here():
    return lax.axis_index("sec") % 2 == 0


def partner(s):
    return s + 1 if s % 2 == 0 else s - 1


def other(s):
    return s - 1 if s % 2 == 0 else s + 1


def places(table, tiles):
    back = reversed_here()
    base = lax.axis_index("sec") * tiles
    sign, flip = jnp.where(back, -1, 1), jnp.where(back, tiles - 1, 0)
    origin = jnp.where(back, tiles - 1 + base, -base)
    return lambda j, p: sign * table[j, sign * p + flip] + origin


def stacked(state, place, p, shift, pairs):
    return jnp.concatenate([state[rows_of(place(j, p) + shift), :] for j in range(pairs)], axis=0)


def product(blocks, state):
    return jnp.dot(blocks, state, preferred_element_type=jnp.float32).astype(jnp.bfloat16)


def blocks_at(parts, cuts, p):
    k = max(k for k in range(len(cuts) - 1) if cuts[k] <= p)
    return parts[k][rows_of(p - cuts[k]), :]


def prepare_edges(pairs, tiles, table, transfer, right):
    bond = right.shape[1]
    starts = [0, tiles - WIDE]

    def kernel(sources, source, environment, first, last, landed, halo, table, arrived, listed):
        back = reversed_here()
        place = places(table, tiles)
        copies = []
        for e, (near, begin) in enumerate(((0, 0), (tiles - REACH, starts[1]))):
            start = jnp.where(back, tiles - REACH - near, near)
            copies.append(pltpu.make_async_copy(source.at[rows_of(start, REACH)], landed.at[rows_of(e * REACH, REACH)], arrived.at[0, e]))
            start = jnp.where(back, tiles - WIDE - begin, begin)
            copies.append(pltpu.make_async_copy(environment.at[rows_of(start, WIDE)], halo.at[rows_of(e * WIDE, WIDE)], arrived.at[1, e]))
        lists = pltpu.make_async_copy(sources, table, listed)
        for copy in [lists, *copies]:
            copy.start()
        first[...] = jnp.zeros_like(first)
        last[...] = jnp.zeros_like(last)
        lists.wait()
        for e, (edge, near) in enumerate(((first, 0), (last, tiles - REACH))):
            copies[2 * e].wait()
            for i in range(REACH):
                p = near + i
                split = jnp.swapaxes(landed[rows_of(e * REACH + jnp.where(back, REACH - 1 - i, i))], 0, 1)
                for j in range(pairs):
                    edge[rows_of(i), rows_of(REACH - place(j, p) + p)] = split[j]
            copies[2 * e + 1].wait()
            for m in range(WIDE):
                at = e * WIDE + jnp.where(back, WIDE - 1 - m, m)
                edge[rows_of(REACH), m * bond : (m + 1) * bond] = halo[rows_of(at), :]

    return pl.pallas_call(
        kernel,
        in_specs=[HBM, HBM, HBM],
        out_specs=[VMEM, VMEM],
        out_shape=[tile_rows(REACH + 1, BAND * TILE)] * 2,
        scratch_shapes=[
            pltpu.VMEM((2 * REACH * TILE, pairs, TILE), jnp.bfloat16),
            pltpu.VMEM((2 * WIDE * TILE, bond), jnp.bfloat16),
            pltpu.SMEM(table.shape, jnp.int32),
            pltpu.SemaphoreType.DMA((2, 2)),
            pltpu.SemaphoreType.DMA,
        ],
        compiler_params=params(),
        cost_estimate=cost(PREPARE / 8),
        name="prepare_edges",
    )(*(pltpu.with_memory_space_constraint(value, pltpu.HBM) for value in (table, transfer, right)))


def prepare(first, final, cuts, pairs, transfer, right):
    tiles, bond = cuts[-1], right.shape[1]
    chosen = range(first, final)
    groups = [(p, min(GROUP, cuts[k + 1] - p)) for k in chosen for p in range(cuts[k], cuts[k + 1], GROUP)]
    begin, end = cuts[first], cuts[final]
    tail = end == tiles

    def kernel(source, environment, *refs):
        parts, refs = refs[: len(chosen)], refs[len(chosen) :]
        landed, arrived, placed = refs[-3:]
        back = reversed_here()
        copies, whole = [], []
        for g, (p, size) in enumerate(groups):
            start = jnp.where(back, tiles - p - size, p)
            copies.append(pltpu.make_async_copy(source.at[rows_of(start, size)], landed.at[rows_of(p - begin, size)], arrived.at[g]))
        if tail:
            for p in range(tiles):
                at = jnp.where(back, tiles - 1 - p, p)
                whole.append(pltpu.make_async_copy(environment.at[rows_of(at)], refs[0].at[rows_of(WIDE + p)], placed.at[p]))
        for copy in copies + whole:
            copy.start()
        for g, (p, size) in enumerate(groups):
            copies[g].wait()
            k = max(k for k in chosen if cuts[k] <= p)
            for i in range(size):
                at = p - begin + jnp.where(back, size - 1 - i, i)
                split = jnp.swapaxes(landed[rows_of(at)], 0, 1)
                for j in range(pairs):
                    parts[k - first][rows_of(p + i - cuts[k]), j * TILE : (j + 1) * TILE] = split[j]
        for copy in whole:
            copy.wait()

    outs = [tile_rows(cuts[k + 1] - cuts[k], pairs * TILE) for k in chosen]
    if tail:
        outs.append(tile_rows(tiles + 2 * WIDE, bond))
    return pl.pallas_call(
        kernel,
        in_specs=[HBM, HBM],
        out_specs=[VMEM] * len(outs),
        out_shape=outs,
        scratch_shapes=[
            pltpu.VMEM(((end - begin) * TILE, pairs, TILE), jnp.bfloat16),
            pltpu.SemaphoreType.DMA((len(groups),)),
            pltpu.SemaphoreType.DMA((tiles,)),
        ],
        compiler_params=params(),
        cost_estimate=cost(PREPARE * (end - begin) / tiles),
        name="prepare",
    )(*(pltpu.with_memory_space_constraint(value, pltpu.HBM) for value in (transfer, right)))


def pair_step(step, k, tiles, pairs, cuts, inner, outer, tables, own, odd, edges, arrived, keeps, give=(), doing=(FILL, EDGE, MAIN), work=0):
    count = len(own)
    head, tail = k == 0, k == count - 1
    edges = (edges[:1] * head + edges[1:] * tail) * (EDGE in doing or step == 0 and FILL in doing)
    arrived = arrived * (FILL in doing)
    bond = keeps[-1].shape[1]
    begin, end = inner[k], inner[k + 1]
    emit = outer is not None and MAIN in doing
    out = (outer[k], outer[k + 1]) if emit else None
    begin_odd, end_odd = 0 if head else begin - REACH, tiles if tail else end - REACH
    odd_parts = [i for i in range(count) if MAIN in doing and cuts[i] < end_odd and cuts[i + 1] > begin_odd]
    own_parts = [i for i in range(count) if emit and cuts[i] < out[1] and cuts[i + 1] > out[0]]
    fixed = [*(own[i] for i in own_parts), *(odd[i] for i in odd_parts), *edges]
    first = 2 + len(fixed) + len(arrived)

    def kernel(table, odd_table, *refs):
        own_refs = dict(zip(own_parts, refs))
        odd_refs = dict(zip(odd_parts, refs[len(own_parts) :]))
        edge_refs = refs[len(own_parts) + len(odd_parts) : len(fixed)]
        came = refs[len(fixed) : first - 2]
        kept, wide, *outs = refs[first - 2 + len(keeps) :]
        kind = kind_here()
        place, odd_place = places(table, tiles), places(odd_table, tiles)

        @pl.when(kind == 2 * step)
        def _():
            if step > 0 and FILL in doing:
                wide[rows_of(WIDE + begin, end - begin), :] = came[0][...]
            for m in range(WIDE * (FILL in doing)):
                if head:
                    value = came[1][rows_of(m), :] if step > 0 else edge_refs[0][rows_of(REACH), m * bond : (m + 1) * bond]
                    wide[rows_of(WIDE - 1 - m), :] = value
                if tail:
                    value = came[-1][rows_of(m), :] if step > 0 else edge_refs[-1][rows_of(REACH), m * bond : (m + 1) * bond]
                    wide[rows_of(tiles + 2 * WIDE - 1 - m), :] = value
            for e in range(REACH * (EDGE in doing)):
                if head:
                    kept[rows_of(REACH - 1 - e), :] = product(edge_refs[0][rows_of(e), :], wide[rows_of(WIDE - 1 - e - REACH, BAND), :])
                if tail:
                    at = tiles + REACH - 1 - e
                    kept[rows_of(REACH + at), :] = product(edge_refs[-1][rows_of(e), :], wide[rows_of(WIDE + at - REACH, BAND), :])
            for p in range(begin_odd, end_odd if MAIN in doing else begin_odd):
                kept[rows_of(REACH + p), :] = product(blocks_at(odd_refs, cuts, p), stacked(wide, odd_place, p, WIDE, pairs))
            for p in range(*(out or (0, 0))):
                fresh = product(blocks_at(own_refs, cuts, p), stacked(kept, place, p, REACH, pairs))
                outs[0][rows_of(p - out[0]), :] = fresh
                if p < WIDE:
                    outs[1][rows_of(p), :] = fresh
                if p >= tiles - WIDE:
                    outs[-1][rows_of(p - (tiles - WIDE)), :] = fresh

        if give:

            @pl.when(kind % 2 == 0)
            def _():
                for (low, high), out in zip(give, outs[len(outs) - len(give) :]):
                    out[...] = wide[rows_of(WIDE + low, high - low), :]

    outs = [tile_rows(tiles + 2 * REACH, bond), tile_rows(tiles + 2 * WIDE, bond)]
    if emit:
        outs += [tile_rows(out[1] - out[0], bond)] + [tile_rows(WIDE, bond)] * (head + tail)
    outs += [tile_rows(high - low, bond) for low, high in give]
    return pl.pallas_call(
        kernel,
        in_specs=[SMEM] * 2 + [VMEM] * (first - 2 + len(keeps)),
        out_specs=[VMEM] * len(outs),
        out_shape=outs,
        input_output_aliases={first + i: 2 - len(keeps) + i for i in range(len(keeps))},
        compiler_params=params(),
        cost_estimate=cost(work or STEP * (end - begin) / tiles),
        name="pair_step",
    )(*tables, *fixed, *arrived, *keeps)


def finish(begin, end, odd_column, tiles, pairs, cuts, table, own, given, regions, left, state, done):
    bond = state.shape[1]
    parts = [k for k in range(len(own)) if cuts[k] < end and cuts[k + 1] > begin]
    groups = [(p, min(GROUP, end - p)) for p in range(begin, end, GROUP)]
    refs_in = [*(own[k] for k in parts), *given, left, state, *done]
    count, fixed = len(parts), len(parts) + len(given) + 2

    def kernel(table, *refs):
        own_refs = dict(zip(parts, refs))
        *taken, rows = refs[count : fixed - 1]
        kept, env, grad, staged_env, staged, sent = refs[len(refs_in) :]

        core = kind_here() % 2

        @pl.when(core == 1)
        def _():
            for (low, high), value in zip(regions, taken):
                kept[rows_of(REACH + low, high - low), :] = value[...]

        @pl.when(core >= 0 if odd_column is None else core == odd_column)
        def _():
            place = places(table, tiles)
            back = reversed_here()
            copies = []
            for g, (p, size) in enumerate(groups):
                start = jnp.where(back, tiles - p - size, p)
                for i in range(size):
                    inside = jnp.where(back, size - 1 - i, i)
                    sources = stacked(kept, place, p + i, REACH, pairs)
                    staged_env[rows_of(p - begin + inside), :] = product(blocks_at(own_refs, cuts, p + i), sources)
                    block = lax.dot_general(
                        rows[rows_of(start + inside), :], sources, (((1,), (1,)), ((), ())), preferred_element_type=jnp.float32
                    ).astype(jnp.bfloat16)
                    block = jnp.stack([block[:, j * TILE : (j + 1) * TILE] for j in range(pairs)], axis=0)
                    staged[rows_of(p - begin + inside)] = jnp.swapaxes(block, 0, 1)
                here, there = rows_of(p - begin, size), rows_of(start, size)
                copies.append(pltpu.make_async_copy(staged_env.at[here], env.at[there], sent.at[0, g]))
                copies.append(pltpu.make_async_copy(staged.at[here], grad.at[there], sent.at[1, g]))
                for copy in copies[-2:]:
                    copy.start()
            for copy in copies:
                copy.wait()

    env = tile_rows(tiles, bond)
    grad = jax.ShapeDtypeStruct((tiles * TILE, pairs, TILE), jnp.bfloat16)
    size = (end - begin) * TILE
    return pl.pallas_call(
        kernel,
        in_specs=[SMEM] + [VMEM] * fixed + [HBM] * len(done),
        out_specs=[VMEM, HBM, HBM],
        out_shape=[tile_rows(tiles + 2 * REACH, bond), env, grad],
        input_output_aliases={fixed + i: i for i in range(1 + len(done))},
        scratch_shapes=[
            pltpu.VMEM((size, bond), jnp.bfloat16),
            pltpu.VMEM((size, pairs, TILE), jnp.bfloat16),
            pltpu.SemaphoreType.DMA((2, len(groups))),
        ],
        compiler_params=params(),
        cost_estimate=cost(FINISH * (end - begin) / tiles),
        name="finish",
    )(table, *refs_in)


def limits(tiles, crossings):
    room = WIDE * crossings
    ends = [e for e in (3 * tiles // 8, 3 * tiles // 4) if room <= e <= tiles - WIDE]
    return ends or [tiles - WIDE]


def per_device(env_right, transfer, sources, env_left):
    ncol, nsec = lax.axis_size("col"), lax.axis_size("sec")
    layers = ncol // 2
    blocks = transfer[0, 0]
    length, pairs = blocks.shape[0], blocks.shape[1]
    tiles = length // TILE
    right, left = env_right[0], env_left[0, 0]

    def move(value, hops):
        both = [(a * nsec + s, b * nsec + to(s)) for a, b, to in hops for s in range(nsec) if 0 <= to(s) < nsec]
        return lax.ppermute(value, ("col", "sec"), both)

    def same(s):
        return s

    swap = [(c, c ^ 1, same) for c in range(ncol)]

    table = sources[0, 0].T

    ends = limits(tiles, layers - 1)
    count = len(ends) + 1
    cuts = [0] + [e + WIDE - REACH for e in ends] + [tiles]
    first_edge, last_edge = prepare_edges(pairs, tiles, table, blocks, right)
    first_edge, last_edge, blocks = lax.optimization_barrier((first_edge, last_edge, blocks))
    (head,) = prepare(0, 1, cuts, pairs, blocks, right)
    *rest, wide = prepare(1, count, cuts, pairs, blocks, right)
    own = [head, *rest]
    odd_cols = [(2 * z + 1, 2 * z) for z in range(layers)]
    odd = [move(part, swap) for part in own]
    odd_table = move(lax.optimization_barrier((table, head))[0], swap)
    odd_edges = [move(first_edge, [(a, b, partner) for a, b in odd_cols]), move(last_edge, [(a, b, other) for a, b in odd_cols])]

    keeps = [wide]
    sent = None
    for step in range(layers):
        end = step == layers - 1
        inner = [0] + [e - WIDE * (step - 1) for e in ends] + [tiles]
        outer = None if end else [0] + [e - WIDE * step for e in ends] + [tiles]
        above, here = 2 * (layers - step), 2 * (layers - 1 - step)
        leaving = []
        for k in range(count):
            came = []
            if step > 0:
                came = [move(sent[k][0], [(above, here, same)])]
                if k == 0:
                    came.append(move(sent[k][1], [(above, here, partner)]))
                if k == count - 1:
                    came.append(halo if end else move(sent[k][-1], [(above, here, other)]))
                if end and k == count - 2:
                    halo = move(sent[k + 1][-1], [(above, here, other)])
                    came.append(halo)
            give = []
            if end and k == count - 2:
                middle = inner[k + 1] // 2
                give = [(-REACH, middle), (middle, inner[k + 1])]
            if end and k == count - 1:
                give = [(inner[k], tiles + REACH)]
            arguments = [table, odd_table], own, odd, odd_edges, came
            if step == 0 and k == 0:
                keeps = pair_step(step, k, tiles, pairs, cuts, inner, None, *arguments, keeps, (), (FILL, EDGE), FIRST)
                result = pair_step(step, k, tiles, pairs, cuts, inner, outer, *arguments, keeps, (), (MAIN,))
            elif end and k == count - 1:
                *keeps, gift = pair_step(step, k, tiles, pairs, cuts, inner, None, *arguments, keeps, give, (FILL,), COLLECT)
                result = pair_step(step, k, tiles, pairs, cuts, inner, None, *arguments, keeps, (), (EDGE, MAIN))
            else:
                result = pair_step(step, k, tiles, pairs, cuts, inner, outer, *arguments, keeps, give, work=SECOND * (step == 0 and k == 1))
            keeps = list(result[:2])
            if give:
                gifts = [gift] if k == count - 1 else result[len(result) - len(give) :]
                given = [move(value, swap) for value in gifts]
                if k == count - 2:
                    half = max(0, give[-1][1] - WIDE) // GROUP * GROUP
                    done = []
                    for odd_column in (0, 1):
                        takes = (given, give) if odd_column else ([], [])
                        keeps[0], *done = finish(0, half, odd_column, tiles, pairs, cuts, table, own, *takes, left, keeps[0], done)
                else:
                    _, env, grad = finish(half, tiles, None, tiles, pairs, cuts, table, own, given, give, left, keeps[0], done)
            leaving.append(result[2:])
        sent = leaving

    return env[None, None], grad[None, None]


def solution(mesh):
    placed = (
        P(None, "sec", None),
        P("col", None, "sec", None, None),
        P("col", None, "sec", None),
        P("col", None, "sec", None),
    )
    return jax.shard_map(
        per_device,
        mesh=mesh,
        in_specs=placed,
        out_specs=(P("col", None, "sec", None), P("col", None, "sec", None, None)),
        check_vma=False,
    )
```

```python
import jax
import jax.numpy as jnp
from jax import lax
from jax.experimental import pallas as pl
from jax.experimental.pallas import tpu as pltpu
from jax.sharding import PartitionSpec as P

TILE = 128
REACH = 2
WIDE = 2 * REACH
BAND = 2 * REACH + 1
GROUP = 4
FILL, EDGE, MAIN = range(3)
PREPARE, FIRST, SECOND, STEP, COLLECT, FINISH = 1e9, 2e10, 2e10, 1e10, 1e9, 4e9
VMEM = pl.BlockSpec(memory_space=pltpu.VMEM)
SMEM = pl.BlockSpec(memory_space=pltpu.SMEM)
HBM = pl.BlockSpec(memory_space=pltpu.HBM)


def params():
    return pltpu.CompilerParams(vmem_limit_bytes=16 * 1024 * 1024)


def cost(flops):
    return pl.CostEstimate(flops=int(flops), bytes_accessed=0, transcendentals=0)


def rows_of(tile, count=1):
    start = tile * TILE
    if not isinstance(start, int):
        start = pl.multiple_of(start, TILE)
    return pl.ds(start, count * TILE)


def tile_rows(count, width):
    return jax.ShapeDtypeStruct((count * TILE, width), jnp.bfloat16)


def kind_here():
    ncol, col = lax.axis_size("col"), lax.axis_index("col")
    return 2 * (ncol // 2 - 1 - col // 2) + col % 2


def reversed_here():
    return lax.axis_index("sec") % 2 == 0


def partner(s):
    return s + 1 if s % 2 == 0 else s - 1


def other(s):
    return s - 1 if s % 2 == 0 else s + 1


def places(table, tiles):
    back = reversed_here()
    base = lax.axis_index("sec") * tiles
    sign, flip = jnp.where(back, -1, 1), jnp.where(back, tiles - 1, 0)
    origin = jnp.where(back, tiles - 1 + base, -base)
    return lambda j, p: sign * table[j, sign * p + flip] + origin


def stacked(state, place, p, shift, pairs):
    return jnp.concatenate([state[rows_of(place(j, p) + shift), :] for j in range(pairs)], axis=0)


def product(blocks, state):
    return jnp.dot(blocks, state, preferred_element_type=jnp.float32).astype(jnp.bfloat16)


def blocks_at(parts, cuts, p):
    k = max(k for k in range(len(cuts) - 1) if cuts[k] <= p)
    return parts[k][rows_of(p - cuts[k]), :]


def prepare_edges(pairs, tiles, table, transfer, right):
    bond = right.shape[1]
    starts = [0, tiles - WIDE]

    def kernel(sources, source, environment, first, last, landed, halo, table, arrived, listed):
        back = reversed_here()
        place = places(table, tiles)
        copies = []
        for e, (near, begin) in enumerate(((0, 0), (tiles - REACH, starts[1]))):
            start = jnp.where(back, tiles - REACH - near, near)
            copies.append(pltpu.make_async_copy(source.at[rows_of(start, REACH)], landed.at[rows_of(e * REACH, REACH)], arrived.at[0, e]))
            start = jnp.where(back, tiles - WIDE - begin, begin)
            copies.append(pltpu.make_async_copy(environment.at[rows_of(start, WIDE)], halo.at[rows_of(e * WIDE, WIDE)], arrived.at[1, e]))
        lists = pltpu.make_async_copy(sources, table, listed)
        for copy in [lists, *copies]:
            copy.start()
        first[...] = jnp.zeros_like(first)
        last[...] = jnp.zeros_like(last)
        lists.wait()
        for e, (edge, near) in enumerate(((first, 0), (last, tiles - REACH))):
            copies[2 * e].wait()
            for i in range(REACH):
                p = near + i
                split = jnp.swapaxes(landed[rows_of(e * REACH + jnp.where(back, REACH - 1 - i, i))], 0, 1)
                for j in range(pairs):
                    edge[rows_of(i), rows_of(REACH - place(j, p) + p)] = split[j]
            copies[2 * e + 1].wait()
            for m in range(WIDE):
                at = e * WIDE + jnp.where(back, WIDE - 1 - m, m)
                edge[rows_of(REACH), m * bond : (m + 1) * bond] = halo[rows_of(at), :]

    return pl.pallas_call(
        kernel,
        in_specs=[HBM, HBM, HBM],
        out_specs=[VMEM, VMEM],
        out_shape=[tile_rows(REACH + 1, BAND * TILE)] * 2,
        scratch_shapes=[
            pltpu.VMEM((2 * REACH * TILE, pairs, TILE), jnp.bfloat16),
            pltpu.VMEM((2 * WIDE * TILE, bond), jnp.bfloat16),
            pltpu.SMEM(table.shape, jnp.int32),
            pltpu.SemaphoreType.DMA((2, 2)),
            pltpu.SemaphoreType.DMA,
        ],
        compiler_params=params(),
        cost_estimate=cost(PREPARE / 8),
        name="prepare_edges",
    )(*(pltpu.with_memory_space_constraint(value, pltpu.HBM) for value in (table, transfer, right)))


def prepare(first, final, cuts, pairs, transfer, right):
    tiles, bond = cuts[-1], right.shape[1]
    chosen = range(first, final)
    groups = [(p, min(GROUP, cuts[k + 1] - p)) for k in chosen for p in range(cuts[k], cuts[k + 1], GROUP)]
    begin, end = cuts[first], cuts[final]
    tail = end == tiles

    def kernel(source, environment, *refs):
        parts, refs = refs[: len(chosen)], refs[len(chosen) :]
        landed, arrived, placed = refs[-3:]
        back = reversed_here()
        copies, whole = [], []
        for g, (p, size) in enumerate(groups):
            start = jnp.where(back, tiles - p - size, p)
            copies.append(pltpu.make_async_copy(source.at[rows_of(start, size)], landed.at[rows_of(p - begin, size)], arrived.at[g]))
        if tail:
            for p in range(tiles):
                at = jnp.where(back, tiles - 1 - p, p)
                whole.append(pltpu.make_async_copy(environment.at[rows_of(at)], refs[0].at[rows_of(WIDE + p)], placed.at[p]))
        for copy in copies + whole:
            copy.start()
        for g, (p, size) in enumerate(groups):
            copies[g].wait()
            k = max(k for k in chosen if cuts[k] <= p)
            for i in range(size):
                at = p - begin + jnp.where(back, size - 1 - i, i)
                split = jnp.swapaxes(landed[rows_of(at)], 0, 1)
                for j in range(pairs):
                    parts[k - first][rows_of(p + i - cuts[k]), j * TILE : (j + 1) * TILE] = split[j]
        for copy in whole:
            copy.wait()

    outs = [tile_rows(cuts[k + 1] - cuts[k], pairs * TILE) for k in chosen]
    if tail:
        outs.append(tile_rows(tiles + 2 * WIDE, bond))
    return pl.pallas_call(
        kernel,
        in_specs=[HBM, HBM],
        out_specs=[VMEM] * len(outs),
        out_shape=outs,
        scratch_shapes=[
            pltpu.VMEM(((end - begin) * TILE, pairs, TILE), jnp.bfloat16),
            pltpu.SemaphoreType.DMA((len(groups),)),
            pltpu.SemaphoreType.DMA((tiles,)),
        ],
        compiler_params=params(),
        cost_estimate=cost(PREPARE * (end - begin) / tiles),
        name="prepare",
    )(*(pltpu.with_memory_space_constraint(value, pltpu.HBM) for value in (transfer, right)))


def pair_step(step, k, tiles, pairs, cuts, inner, outer, tables, own, odd, edges, arrived, keeps, give=(), doing=(FILL, EDGE, MAIN), work=0):
    count = len(own)
    head, tail = k == 0, k == count - 1
    edges = (edges[:1] * head + edges[1:] * tail) * (EDGE in doing or step == 0 and FILL in doing)
    arrived = arrived * (FILL in doing)
    bond = keeps[-1].shape[1]
    begin, end = inner[k], inner[k + 1]
    emit = outer is not None and MAIN in doing
    out = (outer[k], outer[k + 1]) if emit else None
    begin_odd, end_odd = 0 if head else begin - REACH, tiles if tail else end - REACH
    odd_parts = [i for i in range(count) if MAIN in doing and cuts[i] < end_odd and cuts[i + 1] > begin_odd]
    own_parts = [i for i in range(count) if emit and cuts[i] < out[1] and cuts[i + 1] > out[0]]
    fixed = [*(own[i] for i in own_parts), *(odd[i] for i in odd_parts), *edges]
    first = 2 + len(fixed) + len(arrived)

    def kernel(table, odd_table, *refs):
        own_refs = dict(zip(own_parts, refs))
        odd_refs = dict(zip(odd_parts, refs[len(own_parts) :]))
        edge_refs = refs[len(own_parts) + len(odd_parts) : len(fixed)]
        came = refs[len(fixed) : first - 2]
        kept, wide, *outs = refs[first - 2 + len(keeps) :]
        kind = kind_here()
        place, odd_place = places(table, tiles), places(odd_table, tiles)

        @pl.when(kind == 2 * step)
        def _():
            if step > 0 and FILL in doing:
                wide[rows_of(WIDE + begin, end - begin), :] = came[0][...]
            for m in range(WIDE * (FILL in doing)):
                if head:
                    value = came[1][rows_of(m), :] if step > 0 else edge_refs[0][rows_of(REACH), m * bond : (m + 1) * bond]
                    wide[rows_of(WIDE - 1 - m), :] = value
                if tail:
                    value = came[-1][rows_of(m), :] if step > 0 else edge_refs[-1][rows_of(REACH), m * bond : (m + 1) * bond]
                    wide[rows_of(tiles + 2 * WIDE - 1 - m), :] = value
            for e in range(REACH * (EDGE in doing)):
                if head:
                    kept[rows_of(REACH - 1 - e), :] = product(edge_refs[0][rows_of(e), :], wide[rows_of(WIDE - 1 - e - REACH, BAND), :])
                if tail:
                    at = tiles + REACH - 1 - e
                    kept[rows_of(REACH + at), :] = product(edge_refs[-1][rows_of(e), :], wide[rows_of(WIDE + at - REACH, BAND), :])
            for p in range(begin_odd, end_odd if MAIN in doing else begin_odd):
                kept[rows_of(REACH + p), :] = product(blocks_at(odd_refs, cuts, p), stacked(wide, odd_place, p, WIDE, pairs))
            for p in range(*(out or (0, 0))):
                fresh = product(blocks_at(own_refs, cuts, p), stacked(kept, place, p, REACH, pairs))
                outs[0][rows_of(p - out[0]), :] = fresh
                if p < WIDE:
                    outs[1][rows_of(p), :] = fresh
                if p >= tiles - WIDE:
                    outs[-1][rows_of(p - (tiles - WIDE)), :] = fresh

        if give:

            @pl.when(kind % 2 == 0)
            def _():
                for (low, high), out in zip(give, outs[len(outs) - len(give) :]):
                    out[...] = wide[rows_of(WIDE + low, high - low), :]

    outs = [tile_rows(tiles + 2 * REACH, bond), tile_rows(tiles + 2 * WIDE, bond)]
    if emit:
        outs += [tile_rows(out[1] - out[0], bond)] + [tile_rows(WIDE, bond)] * (head + tail)
    outs += [tile_rows(high - low, bond) for low, high in give]
    return pl.pallas_call(
        kernel,
        in_specs=[SMEM] * 2 + [VMEM] * (first - 2 + len(keeps)),
        out_specs=[VMEM] * len(outs),
        out_shape=outs,
        input_output_aliases={first + i: 2 - len(keeps) + i for i in range(len(keeps))},
        compiler_params=params(),
        cost_estimate=cost(work or STEP * (end - begin) / tiles),
        name="pair_step",
    )(*tables, *fixed, *arrived, *keeps)


def finish(begin, end, odd_column, tiles, pairs, cuts, table, own, given, regions, left, state, done, extra=()):
    bond = state.shape[1]
    parts = [k for k in range(len(own)) if cuts[k] < end and cuts[k + 1] > begin]
    groups = [(p, min(GROUP, end - p)) for p in range(begin, end, GROUP)]
    refs_in = [*(own[k] for k in parts), *given, *extra, left, state, *done]
    count, fixed = len(parts), len(parts) + len(given) + len(extra) + 2

    def kernel(table, *refs):
        own_refs = dict(zip(parts, refs))
        *taken, rows = refs[count : fixed - 1]
        kept, env, grad, staged_env, staged, sent = refs[len(refs_in) :]

        core = kind_here() % 2

        @pl.when(core == 1)
        def _():
            for (low, high), value in zip(regions, taken):
                kept[rows_of(REACH + low, high - low), :] = value[...]

        @pl.when(core >= 0 if odd_column is None else core == odd_column)
        def _():
            place = places(table, tiles)
            back = reversed_here()
            copies = []
            for g, (p, size) in enumerate(groups):
                start = jnp.where(back, tiles - p - size, p)
                for i in range(size):
                    inside = jnp.where(back, size - 1 - i, i)
                    sources = stacked(kept, place, p + i, REACH, pairs)
                    staged_env[rows_of(p - begin + inside), :] = product(blocks_at(own_refs, cuts, p + i), sources)
                    block = lax.dot_general(
                        rows[rows_of(start + inside), :], sources, (((1,), (1,)), ((), ())), preferred_element_type=jnp.float32
                    ).astype(jnp.bfloat16)
                    block = jnp.stack([block[:, j * TILE : (j + 1) * TILE] for j in range(pairs)], axis=0)
                    staged[rows_of(p - begin + inside)] = jnp.swapaxes(block, 0, 1)
                here, there = rows_of(p - begin, size), rows_of(start, size)
                copies.append(pltpu.make_async_copy(staged_env.at[here], env.at[there], sent.at[0, g]))
                copies.append(pltpu.make_async_copy(staged.at[here], grad.at[there], sent.at[1, g]))
                for copy in copies[-2:]:
                    copy.start()
            for copy in copies:
                copy.wait()

    env = tile_rows(tiles, bond)
    grad = jax.ShapeDtypeStruct((tiles * TILE, pairs, TILE), jnp.bfloat16)
    size = (end - begin) * TILE
    return pl.pallas_call(
        kernel,
        in_specs=[SMEM] + [VMEM] * fixed + [HBM] * len(done),
        out_specs=[VMEM, HBM, HBM],
        out_shape=[tile_rows(tiles + 2 * REACH, bond), env, grad],
        input_output_aliases={fixed + i: i for i in range(1 + len(done))},
        scratch_shapes=[
            pltpu.VMEM((size, bond), jnp.bfloat16),
            pltpu.VMEM((size, pairs, TILE), jnp.bfloat16),
            pltpu.SemaphoreType.DMA((2, len(groups))),
        ],
        compiler_params=params(),
        cost_estimate=cost(FINISH if odd_column == 0 else FINISH * (end - begin) / tiles),
        name="finish",
    )(table, *refs_in)


def limits(tiles, crossings):
    room = WIDE * crossings
    ends = [e for e in (3 * tiles // 8, 3 * tiles // 4) if room <= e <= tiles - WIDE]
    return ends or [tiles - WIDE]


def per_device(env_right, transfer, sources, env_left):
    ncol, nsec = lax.axis_size("col"), lax.axis_size("sec")
    layers = ncol // 2
    blocks = transfer[0, 0]
    length, pairs = blocks.shape[0], blocks.shape[1]
    tiles = length // TILE
    right, left = env_right[0], env_left[0, 0]

    def move(value, hops):
        both = [(a * nsec + s, b * nsec + to(s)) for a, b, to in hops for s in range(nsec) if 0 <= to(s) < nsec]
        return lax.ppermute(value, ("col", "sec"), both)

    def same(s):
        return s

    swap = [(c, c ^ 1, same) for c in range(ncol)]

    table = sources[0, 0].T

    ends = limits(tiles, layers - 1)
    count = len(ends) + 1
    cuts = [0] + [e + WIDE - REACH for e in ends] + [tiles]
    first_edge, last_edge = prepare_edges(pairs, tiles, table, blocks, right)
    first_edge, last_edge, blocks = lax.optimization_barrier((first_edge, last_edge, blocks))
    (head,) = prepare(0, 1, cuts, pairs, blocks, right)
    *rest, wide = prepare(1, count, cuts, pairs, blocks, right)
    own = [head, *rest]
    odd_cols = [(2 * z + 1, 2 * z) for z in range(layers)]
    odd = [move(part, swap) for part in own]
    listed, _ = lax.optimization_barrier((table, head))
    odd_table = move(listed, swap)
    odd_edges = [move(first_edge, [(a, b, partner) for a, b in odd_cols]), move(last_edge, [(a, b, other) for a, b in odd_cols])]

    keeps = [wide]
    sent = None
    for step in range(layers):
        end = step == layers - 1
        inner = [0] + [e - WIDE * (step - 1) for e in ends] + [tiles]
        outer = None if end else [0] + [e - WIDE * step for e in ends] + [tiles]
        above, here = 2 * (layers - step), 2 * (layers - 1 - step)
        leaving = []
        for k in range(count):
            came = []
            if step > 0:
                came = [move(sent[k][0], [(above, here, same)])]
                if k == 0:
                    came.append(move(sent[k][1], [(above, here, partner)]))
                if k == count - 1:
                    came.append(halo if end else move(sent[k][-1], [(above, here, other)]))
                if end and k == count - 2:
                    halo = move(sent[k + 1][-1], [(above, here, other)])
            give = []
            if end and k == count - 2:
                middle = inner[k + 1] // 2
                give = [(-REACH, middle), (middle, inner[k + 1])]
            if end and k == count - 1:
                give = [(inner[k], tiles + REACH)]
            arguments = [table, odd_table], own, odd, odd_edges, came
            if step == 0 and k == 0:
                keeps = pair_step(step, k, tiles, pairs, cuts, inner, None, *arguments, keeps, (), (FILL, EDGE), FIRST)
                result = pair_step(step, k, tiles, pairs, cuts, inner, outer, *arguments, keeps, (), (MAIN,))
            elif end and k == count - 1:
                *keeps, gift = pair_step(step, k, tiles, pairs, cuts, inner, None, *arguments, keeps, give, (FILL,), COLLECT)
                result = pair_step(step, k, tiles, pairs, cuts, inner, None, *arguments, keeps, (), (EDGE, MAIN))
            else:
                result = pair_step(step, k, tiles, pairs, cuts, inner, outer, *arguments, keeps, give, work=SECOND * (step == 0 and k == 1))
            keeps = list(result[:2])
            if give:
                gifts = [gift] if k == count - 1 else result[len(result) - len(give) :]
                given = [move(value, swap) for value in gifts]
                if k == count - 2:
                    half = max(0, give[-1][1] - WIDE) // GROUP * GROUP
                    done = []
                    for odd_column in (0, 1):
                        takes = (given, give) if odd_column else ([], [])
                        extra = [] if odd_column else [halo]
                        keeps[0], *done = finish(0, half, odd_column, tiles, pairs, cuts, table, own, *takes, left, keeps[0], done, extra)
                else:
                    _, env, grad = finish(half, tiles, None, tiles, pairs, cuts, table, own, given, give, left, keeps[0], done)
            leaving.append(result[2:])
        sent = leaving

    return env[None, None], grad[None, None]


def solution(mesh):
    placed = (
        P(None, "sec", None),
        P("col", None, "sec", None, None),
        P("col", None, "sec", None),
        P("col", None, "sec", None),
    )
    return jax.shard_map(
        per_device,
        mesh=mesh,
        in_specs=placed,
        out_specs=(P("col", None, "sec", None), P("col", None, "sec", None, None)),
        check_vma=False,
    )
```

```python
import jax
import jax.numpy as jnp
from jax import lax
from jax.experimental import pallas as pl
from jax.experimental.pallas import tpu as pltpu
from jax.sharding import PartitionSpec as P

TILE = 128
REACH = 2
WIDE = 2 * REACH
BAND = 2 * REACH + 1
GROUP = 4
FILL, EDGE, MAIN = range(3)
PREPARE, FIRST, SECOND, STEP, COLLECT, FINISH = 1e9, 2e10, 2e10, 1e10, 1e9, 4e9
VMEM = pl.BlockSpec(memory_space=pltpu.VMEM)
HBM = pl.BlockSpec(memory_space=pltpu.HBM)
ANY = pl.BlockSpec(memory_space=pl.ANY)


def params():
    return pltpu.CompilerParams(vmem_limit_bytes=16 * 1024 * 1024)


def cost(flops):
    return pl.CostEstimate(flops=int(flops), bytes_accessed=0, transcendentals=0)


def rows_of(tile, count=1):
    start = tile * TILE
    if not isinstance(start, int):
        start = pl.multiple_of(start, TILE)
    return pl.ds(start, count * TILE)


def tile_rows(count, width):
    return jax.ShapeDtypeStruct((count * TILE, width), jnp.bfloat16)


def kind_here():
    ncol, col = lax.axis_size("col"), lax.axis_index("col")
    return 2 * (ncol // 2 - 1 - col // 2) + col % 2


def reversed_here():
    return lax.axis_index("sec") % 2 == 0


def partner(s):
    return s + 1 if s % 2 == 0 else s - 1


def other(s):
    return s - 1 if s % 2 == 0 else s + 1


def places(table, tiles):
    back = reversed_here()
    base = lax.axis_index("sec") * tiles
    sign, flip = jnp.where(back, -1, 1), jnp.where(back, tiles - 1, 0)
    origin = jnp.where(back, tiles - 1 + base, -base)
    return lambda j, p: sign * table[j, sign * p + flip] + origin


def stacked(state, place, p, shift, pairs):
    return jnp.concatenate([state[rows_of(place(j, p) + shift), :] for j in range(pairs)], axis=0)


def product(blocks, state):
    return jnp.dot(blocks, state, preferred_element_type=jnp.float32).astype(jnp.bfloat16)


def blocks_at(parts, cuts, p):
    k = max(k for k in range(len(cuts) - 1) if cuts[k] <= p)
    return parts[k][rows_of(p - cuts[k]), :]


def prepare_edges(pairs, tiles, table, transfer, right):
    bond = right.shape[1]
    starts = [0, tiles - WIDE]

    def kernel(sources, source, environment, first, last, landed, halo, table, arrived, listed):
        back = reversed_here()
        place = places(table, tiles)
        copies = []
        for e, (near, begin) in enumerate(((0, 0), (tiles - REACH, starts[1]))):
            start = jnp.where(back, tiles - REACH - near, near)
            copies.append(pltpu.make_async_copy(source.at[rows_of(start, REACH)], landed.at[rows_of(e * REACH, REACH)], arrived.at[0, e]))
            start = jnp.where(back, tiles - WIDE - begin, begin)
            copies.append(pltpu.make_async_copy(environment.at[rows_of(start, WIDE)], halo.at[rows_of(e * WIDE, WIDE)], arrived.at[1, e]))
        lists = pltpu.make_async_copy(sources, table, listed)
        for copy in [lists, *copies]:
            copy.start()
        first[...] = jnp.zeros_like(first)
        last[...] = jnp.zeros_like(last)
        lists.wait()
        for e, (edge, near) in enumerate(((first, 0), (last, tiles - REACH))):
            copies[2 * e].wait()
            for i in range(REACH):
                p = near + i
                split = jnp.swapaxes(landed[rows_of(e * REACH + jnp.where(back, REACH - 1 - i, i))], 0, 1)
                for j in range(pairs):
                    edge[rows_of(i), rows_of(REACH - place(j, p) + p)] = split[j]
            copies[2 * e + 1].wait()
            for m in range(WIDE):
                at = e * WIDE + jnp.where(back, WIDE - 1 - m, m)
                edge[rows_of(REACH), m * bond : (m + 1) * bond] = halo[rows_of(at), :]

    return pl.pallas_call(
        kernel,
        in_specs=[HBM, HBM, HBM],
        out_specs=[VMEM, VMEM],
        out_shape=[tile_rows(REACH + 1, BAND * TILE)] * 2,
        scratch_shapes=[
            pltpu.VMEM((2 * REACH * TILE, pairs, TILE), jnp.bfloat16),
            pltpu.VMEM((2 * WIDE * TILE, bond), jnp.bfloat16),
            pltpu.SMEM(table.shape, jnp.int32),
            pltpu.SemaphoreType.DMA((2, 2)),
            pltpu.SemaphoreType.DMA,
        ],
        compiler_params=params(),
        cost_estimate=cost(PREPARE / 8),
        name="prepare_edges",
    )(*(pltpu.with_memory_space_constraint(value, pltpu.HBM) for value in (table, transfer, right)))


def prepare(first, final, cuts, pairs, transfer, right):
    tiles, bond = cuts[-1], right.shape[1]
    chosen = range(first, final)
    groups = [(p, min(GROUP, cuts[k + 1] - p)) for k in chosen for p in range(cuts[k], cuts[k + 1], GROUP)]
    begin, end = cuts[first], cuts[final]
    with_environment = first == 0

    def kernel(source, environment, *refs):
        parts, refs = refs[: len(chosen)], refs[len(chosen) :]
        landed, arrived, placed = refs[-3:]
        back = reversed_here()
        copies, whole = [], []
        for g, (p, size) in enumerate(groups):
            start = jnp.where(back, tiles - p - size, p)
            copies.append(pltpu.make_async_copy(source.at[rows_of(start, size)], landed.at[rows_of(p - begin, size)], arrived.at[g]))
        if with_environment:
            for p in range(tiles):
                at = jnp.where(back, tiles - 1 - p, p)
                whole.append(pltpu.make_async_copy(environment.at[rows_of(at)], refs[0].at[rows_of(WIDE + p)], placed.at[p]))
        for copy in copies + whole:
            copy.start()
        for g, (p, size) in enumerate(groups):
            copies[g].wait()
            k = max(k for k in chosen if cuts[k] <= p)
            for i in range(size):
                at = p - begin + jnp.where(back, size - 1 - i, i)
                split = jnp.swapaxes(landed[rows_of(at)], 0, 1)
                for j in range(pairs):
                    parts[k - first][rows_of(p + i - cuts[k]), j * TILE : (j + 1) * TILE] = split[j]
        for copy in whole:
            copy.wait()

    outs = [tile_rows(cuts[k + 1] - cuts[k], pairs * TILE) for k in chosen]
    if with_environment:
        outs.append(tile_rows(tiles + 2 * WIDE, bond))
    return pl.pallas_call(
        kernel,
        in_specs=[HBM, HBM],
        out_specs=[VMEM] * len(outs),
        out_shape=outs,
        scratch_shapes=[
            pltpu.VMEM(((end - begin) * TILE, pairs, TILE), jnp.bfloat16),
            pltpu.SemaphoreType.DMA((len(groups),)),
            pltpu.SemaphoreType.DMA((tiles,)),
        ],
        compiler_params=params(),
        cost_estimate=cost(PREPARE * (end - begin) / tiles),
        name="prepare",
    )(*(pltpu.with_memory_space_constraint(value, pltpu.HBM) for value in (transfer, right)))


def pair_step(step, k, tiles, pairs, cuts, inner, outer, tables, own, odd, edges, arrived, keeps, give=(), doing=(FILL, EDGE, MAIN), work=0):
    count = len(cuts) - 1
    head, tail = k == 0, k == count - 1
    edges = (edges[:1] * head + edges[1:] * tail) * (EDGE in doing or step == 0 and FILL in doing)
    arrived = arrived * (FILL in doing)
    bond = keeps[-1].shape[1]
    begin, end = inner[k], inner[k + 1]
    emit = outer is not None and MAIN in doing
    out = (outer[k], outer[k + 1]) if emit else None
    begin_odd, end_odd = 0 if head else begin - REACH, tiles if tail else end - REACH
    odd_parts = [i for i in range(count) if MAIN in doing and cuts[i] < end_odd and cuts[i + 1] > begin_odd]
    own_parts = [i for i in range(count) if emit and cuts[i] < out[1] and cuts[i + 1] > out[0]]
    fixed = [*(own[i] for i in own_parts), *(odd[i] for i in odd_parts), *edges]
    first = 2 + len(fixed) + len(arrived)

    def kernel(own_list, odd_list, *refs):
        *refs, table, odd_table, listed = refs
        own_refs = dict(zip(own_parts, refs))
        odd_refs = dict(zip(odd_parts, refs[len(own_parts) :]))
        edge_refs = refs[len(own_parts) + len(odd_parts) : len(fixed)]
        came = refs[len(fixed) : first - 2]
        kept, wide, *outs = refs[first - 2 + len(keeps) :]
        kind = kind_here()
        place, odd_place = places(table, tiles), places(odd_table, tiles)

        @pl.when(kind == 2 * step)
        def _():
            lists = []
            if MAIN in doing:
                lists = [pltpu.make_async_copy(own_list, table, listed.at[0]), pltpu.make_async_copy(odd_list, odd_table, listed.at[1])]
            for copy in lists:
                copy.start()
            if step > 0 and FILL in doing:
                wide[rows_of(WIDE + begin, end - begin), :] = came[0][...]
            for m in range(WIDE * (FILL in doing)):
                if head:
                    value = came[1][rows_of(m), :] if step > 0 else edge_refs[0][rows_of(REACH), m * bond : (m + 1) * bond]
                    wide[rows_of(WIDE - 1 - m), :] = value
                if tail:
                    value = came[-1][rows_of(m), :] if step > 0 else edge_refs[-1][rows_of(REACH), m * bond : (m + 1) * bond]
                    wide[rows_of(tiles + 2 * WIDE - 1 - m), :] = value
            for e in range(REACH * (EDGE in doing)):
                if head:
                    kept[rows_of(REACH - 1 - e), :] = product(edge_refs[0][rows_of(e), :], wide[rows_of(WIDE - 1 - e - REACH, BAND), :])
                if tail:
                    at = tiles + REACH - 1 - e
                    kept[rows_of(REACH + at), :] = product(edge_refs[-1][rows_of(e), :], wide[rows_of(WIDE + at - REACH, BAND), :])
            for copy in lists:
                copy.wait()
            for p in range(begin_odd, end_odd if MAIN in doing else begin_odd):
                kept[rows_of(REACH + p), :] = product(blocks_at(odd_refs, cuts, p), stacked(wide, odd_place, p, WIDE, pairs))
            for p in range(*(out or (0, 0))):
                fresh = product(blocks_at(own_refs, cuts, p), stacked(kept, place, p, REACH, pairs))
                outs[0][rows_of(p - out[0]), :] = fresh
                if p < WIDE:
                    outs[1][rows_of(p), :] = fresh
                if p >= tiles - WIDE:
                    outs[-1][rows_of(p - (tiles - WIDE)), :] = fresh

        if give:

            @pl.when(kind % 2 == 0)
            def _():
                for (low, high), out in zip(give, outs[len(outs) - len(give) :]):
                    out[...] = wide[rows_of(WIDE + low, high - low), :]

    outs = [tile_rows(tiles + 2 * REACH, bond), tile_rows(tiles + 2 * WIDE, bond)]
    if emit:
        outs += [tile_rows(out[1] - out[0], bond)] + [tile_rows(WIDE, bond)] * (head + tail)
    outs += [tile_rows(high - low, bond) for low, high in give]
    return pl.pallas_call(
        kernel,
        in_specs=[ANY] * 2 + [VMEM] * (first - 2 + len(keeps)),
        out_specs=[VMEM] * len(outs),
        out_shape=outs,
        input_output_aliases={first + i: 2 - len(keeps) + i for i in range(len(keeps))},
        scratch_shapes=[pltpu.SMEM(tables[0].shape, jnp.int32)] * 2 + [pltpu.SemaphoreType.DMA((2,))],
        compiler_params=params(),
        cost_estimate=cost(work or STEP * (end - begin) / tiles),
        name="pair_step",
    )(*tables, *fixed, *arrived, *keeps)


def finish(begin, end, odd_column, tiles, pairs, cuts, table, own, given, regions, left, state, done, extra=()):
    bond = state.shape[1]
    parts = [k for k in range(len(own)) if cuts[k] < end and cuts[k + 1] > begin]
    limit = max(begin, end - GROUP)
    groups = [(p, min(GROUP, limit - p)) for p in range(begin, limit, GROUP)] + [(p, 1) for p in range(limit, end)]
    refs_in = [*(own[k] for k in parts), *given, *extra, left, state, *done]
    count, fixed = len(parts), len(parts) + len(given) + len(extra) + 2

    def kernel(own_list, *refs):
        own_refs = dict(zip(parts, refs))
        *taken, rows = refs[count : fixed - 1]
        kept, env, grad, staged_env, staged, sent, table, listed = refs[len(refs_in) :]

        core = kind_here() % 2
        lists = pltpu.make_async_copy(own_list, table, listed)

        @pl.when(core == 1)
        def _():
            for (low, high), value in zip(regions, taken):
                kept[rows_of(REACH + low, high - low), :] = value[...]

        @pl.when(core >= 0 if odd_column is None else core == odd_column)
        def _():
            lists.start()
            lists.wait()
            place = places(table, tiles)
            back = reversed_here()
            copies = []
            for g, (p, size) in enumerate(groups):
                start = jnp.where(back, tiles - p - size, p)
                for i in range(size):
                    inside = jnp.where(back, size - 1 - i, i)
                    sources = stacked(kept, place, p + i, REACH, pairs)
                    staged_env[rows_of(p - begin + inside), :] = product(blocks_at(own_refs, cuts, p + i), sources)
                    block = lax.dot_general(
                        rows[rows_of(start + inside), :], sources, (((1,), (1,)), ((), ())), preferred_element_type=jnp.float32
                    ).astype(jnp.bfloat16)
                    block = jnp.stack([block[:, j * TILE : (j + 1) * TILE] for j in range(pairs)], axis=0)
                    staged[rows_of(p - begin + inside)] = jnp.swapaxes(block, 0, 1)
                here, there = rows_of(p - begin, size), rows_of(start, size)
                copies.append(pltpu.make_async_copy(staged_env.at[here], env.at[there], sent.at[0, g]))
                copies.append(pltpu.make_async_copy(staged.at[here], grad.at[there], sent.at[1, g]))
                for copy in copies[-2:]:
                    copy.start()
            for copy in copies:
                copy.wait()

    env = tile_rows(tiles, bond)
    grad = jax.ShapeDtypeStruct((tiles * TILE, pairs, TILE), jnp.bfloat16)
    size = (end - begin) * TILE
    return pl.pallas_call(
        kernel,
        in_specs=[ANY] + [VMEM] * fixed + [HBM] * len(done),
        out_specs=[VMEM, HBM, HBM],
        out_shape=[tile_rows(tiles + 2 * REACH, bond), env, grad],
        input_output_aliases={fixed + i: i for i in range(1 + len(done))},
        scratch_shapes=[
            pltpu.VMEM((size, bond), jnp.bfloat16),
            pltpu.VMEM((size, pairs, TILE), jnp.bfloat16),
            pltpu.SemaphoreType.DMA((2, len(groups))),
            pltpu.SMEM(table.shape, jnp.int32),
            pltpu.SemaphoreType.DMA,
        ],
        compiler_params=params(),
        cost_estimate=cost(FINISH if odd_column == 0 else FINISH * (end - begin) / tiles),
        name="finish",
    )(table, *refs_in)


def limits(tiles, crossings):
    room = WIDE * crossings
    ends = [e for e in (3 * tiles // 8, 3 * tiles // 4) if room <= e <= tiles - WIDE]
    return ends or [tiles - WIDE]


def per_device(env_right, transfer, sources, env_left):
    ncol, nsec = lax.axis_size("col"), lax.axis_size("sec")
    layers = ncol // 2
    blocks = transfer[0, 0]
    length, pairs = blocks.shape[0], blocks.shape[1]
    tiles = length // TILE
    right, left = env_right[0], env_left[0, 0]

    def move(value, hops):
        both = [(a * nsec + s, b * nsec + to(s)) for a, b, to in hops for s in range(nsec) if 0 <= to(s) < nsec]
        return lax.ppermute(value, ("col", "sec"), both)

    def same(s):
        return s

    swap = [(c, c ^ 1, same) for c in range(ncol)]

    table = sources[0, 0].T

    ends = limits(tiles, layers - 1)
    count = len(ends) + 1
    cuts = [0] + [e + WIDE - REACH for e in ends] + [tiles]
    first_edge, last_edge = prepare_edges(pairs, tiles, table, blocks, right)
    first_edge, last_edge, blocks = lax.optimization_barrier((first_edge, last_edge, blocks))
    head, wide = prepare(0, 1, cuts, pairs, blocks, right)
    middle = prepare(1, count - 1, cuts, pairs, blocks, right) if count > 2 else []
    own = [head, *middle]
    odd_cols = [(2 * z + 1, 2 * z) for z in range(layers)]
    odd = [move(part, swap) for part in own]
    listed, _ = lax.optimization_barrier((table, head))
    odd_table = move(listed, swap)
    last_edge, _ = lax.optimization_barrier((last_edge, own[-1]))
    odd_edges = [move(first_edge, [(a, b, partner) for a, b in odd_cols]), move(last_edge, [(a, b, other) for a, b in odd_cols])]

    keeps = [wide]
    sent = None
    for step in range(layers):
        end = step == layers - 1
        inner = [0] + [e - WIDE * (step - 1) for e in ends] + [tiles]
        outer = None if end else [0] + [e - WIDE * step for e in ends] + [tiles]
        above, here = 2 * (layers - step), 2 * (layers - 1 - step)
        leaving = []
        for k in range(count):
            came = []
            if step > 0:
                came = [move(sent[k][0], [(above, here, same)])]
                if k == 0:
                    came.append(move(sent[k][1], [(above, here, partner)]))
                if k == count - 1:
                    came.append(halo if end else move(sent[k][-1], [(above, here, other)]))
                if end and k == count - 2:
                    halo = move(sent[k + 1][-1], [(above, here, other)])
            give = []
            if end and k == count - 2:
                middle = inner[k + 1] // 2
                give = [(-REACH, middle), (middle, inner[k + 1])]
            if end and k == count - 1:
                give = [(inner[k], tiles + REACH)]
            arguments = [table, odd_table], own, odd, odd_edges, came
            if step == 0 and k == 0:
                keeps = pair_step(step, k, tiles, pairs, cuts, inner, None, *arguments, keeps, (), (FILL, EDGE), FIRST)
                result = pair_step(step, k, tiles, pairs, cuts, inner, outer, *arguments, keeps, (), (MAIN,))
                own += prepare(count - 1, count, cuts, pairs, lax.optimization_barrier((blocks, result[2]))[0], right)
                odd.append(move(own[-1], swap))
            elif end and k == count - 1:
                *keeps, gift = pair_step(step, k, tiles, pairs, cuts, inner, None, *arguments, keeps, give, (FILL,), COLLECT)
                result = pair_step(step, k, tiles, pairs, cuts, inner, None, *arguments, keeps, (), (EDGE, MAIN))
            else:
                result = pair_step(step, k, tiles, pairs, cuts, inner, outer, *arguments, keeps, give, work=SECOND * (step == 0 and k == 1))
            keeps = list(result[:2])
            if give:
                gifts = [gift] if k == count - 1 else result[len(result) - len(give) :]
                given = [move(value, swap) for value in gifts]
                if k == count - 2:
                    half = max(0, give[-1][1] - WIDE) // GROUP * GROUP
                    done = []
                    for odd_column in (0, 1):
                        takes = (given, give) if odd_column else ([], [])
                        extra = [] if odd_column else [halo]
                        keeps[0], *done = finish(0, half, odd_column, tiles, pairs, cuts, table, own, *takes, left, keeps[0], done, extra)
                else:
                    _, env, grad = finish(half, tiles, None, tiles, pairs, cuts, table, own, given, give, left, keeps[0], done)
            leaving.append(result[2:])
        sent = leaving

    return env[None, None], grad[None, None]


def solution(mesh):
    placed = (
        P(None, "sec", None),
        P("col", None, "sec", None, None),
        P("col", None, "sec", None),
        P("col", None, "sec", None),
    )
    return jax.shard_map(
        per_device,
        mesh=mesh,
        in_specs=placed,
        out_specs=(P("col", None, "sec", None), P("col", None, "sec", None, None)),
        check_vma=False,
    )
```

```python
import jax
import jax.numpy as jnp
from jax import lax
from jax.experimental import pallas as pl
from jax.experimental.pallas import tpu as pltpu
from jax.sharding import PartitionSpec as P

TILE = 128
REACH = 2
WIDE = 2 * REACH
BAND = 2 * REACH + 1
GROUP = 4
FILL, EDGE, MAIN = range(3)
PREPARE, FIRST, SECOND, STEP, COLLECT, FINISH = 1e9, 2e10, 2e10, 1e10, 1e9, 4e9
VMEM = pl.BlockSpec(memory_space=pltpu.VMEM)
HBM = pl.BlockSpec(memory_space=pltpu.HBM)
ANY = pl.BlockSpec(memory_space=pl.ANY)


def params():
    return pltpu.CompilerParams(vmem_limit_bytes=16 * 1024 * 1024)


def cost(flops):
    return pl.CostEstimate(flops=int(flops), bytes_accessed=0, transcendentals=0)


def rows_of(tile, count=1):
    start = tile * TILE
    if not isinstance(start, int):
        start = pl.multiple_of(start, TILE)
    return pl.ds(start, count * TILE)


def tile_rows(count, width):
    return jax.ShapeDtypeStruct((count * TILE, width), jnp.bfloat16)


def kind_here():
    ncol, col = lax.axis_size("col"), lax.axis_index("col")
    return 2 * (ncol // 2 - 1 - col // 2) + col % 2


def reversed_here():
    return lax.axis_index("sec") % 2 == 0


def partner(s):
    return s + 1 if s % 2 == 0 else s - 1


def other(s):
    return s - 1 if s % 2 == 0 else s + 1


def places(table, tiles):
    back = reversed_here()
    base = lax.axis_index("sec") * tiles
    sign, flip = jnp.where(back, -1, 1), jnp.where(back, tiles - 1, 0)
    origin = jnp.where(back, tiles - 1 + base, -base)
    return lambda j, p: sign * table[j, sign * p + flip] + origin


def stacked(state, place, p, shift, pairs):
    return jnp.concatenate([state[rows_of(place(j, p) + shift), :] for j in range(pairs)], axis=0)


def product(blocks, state):
    return jnp.dot(blocks, state, preferred_element_type=jnp.float32).astype(jnp.bfloat16)


def blocks_at(parts, cuts, p):
    k = max(k for k in range(len(cuts) - 1) if cuts[k] <= p)
    return parts[k][rows_of(p - cuts[k]), :]


def prepare_edges(pairs, tiles, table, transfer, right):
    bond = right.shape[1]
    starts = [0, tiles - WIDE]

    def kernel(sources, source, environment, first, last, landed, halo, table, arrived, listed):
        back = reversed_here()
        place = places(table, tiles)
        copies = []
        for e, (near, begin) in enumerate(((0, 0), (tiles - REACH, starts[1]))):
            start = jnp.where(back, tiles - REACH - near, near)
            copies.append(pltpu.make_async_copy(source.at[rows_of(start, REACH)], landed.at[rows_of(e * REACH, REACH)], arrived.at[0, e]))
            start = jnp.where(back, tiles - WIDE - begin, begin)
            copies.append(pltpu.make_async_copy(environment.at[rows_of(start, WIDE)], halo.at[rows_of(e * WIDE, WIDE)], arrived.at[1, e]))
        lists = pltpu.make_async_copy(sources, table, listed)
        for copy in [lists, *copies]:
            copy.start()
        first[...] = jnp.zeros_like(first)
        last[...] = jnp.zeros_like(last)
        lists.wait()
        for e, (edge, near) in enumerate(((first, 0), (last, tiles - REACH))):
            copies[2 * e].wait()
            for i in range(REACH):
                p = near + i
                split = jnp.swapaxes(landed[rows_of(e * REACH + jnp.where(back, REACH - 1 - i, i))], 0, 1)
                for j in range(pairs):
                    edge[rows_of(i), rows_of(REACH - place(j, p) + p)] = split[j]
            copies[2 * e + 1].wait()
            for m in range(WIDE):
                at = e * WIDE + jnp.where(back, WIDE - 1 - m, m)
                edge[rows_of(REACH), m * bond : (m + 1) * bond] = halo[rows_of(at), :]

    return pl.pallas_call(
        kernel,
        in_specs=[HBM, HBM, HBM],
        out_specs=[VMEM, VMEM],
        out_shape=[tile_rows(REACH + 1, BAND * TILE)] * 2,
        scratch_shapes=[
            pltpu.VMEM((2 * REACH * TILE, pairs, TILE), jnp.bfloat16),
            pltpu.VMEM((2 * WIDE * TILE, bond), jnp.bfloat16),
            pltpu.SMEM(table.shape, jnp.int32),
            pltpu.SemaphoreType.DMA((2, 2)),
            pltpu.SemaphoreType.DMA,
        ],
        compiler_params=params(),
        cost_estimate=cost(PREPARE / 8),
        name="prepare_edges",
    )(*(pltpu.with_memory_space_constraint(value, pltpu.HBM) for value in (table, transfer, right)))


def prepare(first, final, cuts, pairs, transfer, right):
    tiles, bond = cuts[-1], right.shape[1]
    chosen = range(first, final)
    groups = [(p, min(GROUP, cuts[k + 1] - p)) for k in chosen for p in range(cuts[k], cuts[k + 1], GROUP)]
    begin, end = cuts[first], cuts[final]
    with_environment = first == 0

    def kernel(source, environment, *refs):
        parts, refs = refs[: len(chosen)], refs[len(chosen) :]
        landed, arrived, placed = refs[-3:]
        back = reversed_here()
        copies, whole = [], []
        for g, (p, size) in enumerate(groups):
            start = jnp.where(back, tiles - p - size, p)
            copies.append(pltpu.make_async_copy(source.at[rows_of(start, size)], landed.at[rows_of(p - begin, size)], arrived.at[g]))
        if with_environment:
            for p in range(tiles):
                at = jnp.where(back, tiles - 1 - p, p)
                whole.append(pltpu.make_async_copy(environment.at[rows_of(at)], refs[0].at[rows_of(WIDE + p)], placed.at[p]))
        for copy in copies + whole:
            copy.start()
        for g, (p, size) in enumerate(groups):
            copies[g].wait()
            k = max(k for k in chosen if cuts[k] <= p)
            for i in range(size):
                at = p - begin + jnp.where(back, size - 1 - i, i)
                split = jnp.swapaxes(landed[rows_of(at)], 0, 1)
                for j in range(pairs):
                    parts[k - first][rows_of(p + i - cuts[k]), j * TILE : (j + 1) * TILE] = split[j]
        for copy in whole:
            copy.wait()

    outs = [tile_rows(cuts[k + 1] - cuts[k], pairs * TILE) for k in chosen]
    if with_environment:
        outs.append(tile_rows(tiles + 2 * WIDE, bond))
    return pl.pallas_call(
        kernel,
        in_specs=[HBM, HBM],
        out_specs=[VMEM] * len(outs),
        out_shape=outs,
        scratch_shapes=[
            pltpu.VMEM(((end - begin) * TILE, pairs, TILE), jnp.bfloat16),
            pltpu.SemaphoreType.DMA((len(groups),)),
            pltpu.SemaphoreType.DMA((tiles,)),
        ],
        compiler_params=params(),
        cost_estimate=cost(PREPARE * (end - begin) / tiles),
        name="prepare",
    )(*(pltpu.with_memory_space_constraint(value, pltpu.HBM) for value in (transfer, right)))


def pair_step(step, k, tiles, pairs, cuts, inner, outer, tables, own, odd, edges, arrived, keeps, give=(), doing=(FILL, EDGE, MAIN), work=0):
    count = len(cuts) - 1
    head, tail = k == 0, k == count - 1
    edges = (edges[:1] * head + edges[1:] * tail) * (EDGE in doing or step == 0 and FILL in doing)
    arrived = arrived * (FILL in doing)
    bond = keeps[-1].shape[1]
    begin, end = inner[k], inner[k + 1]
    emit = outer is not None and MAIN in doing
    out = (outer[k], outer[k + 1]) if emit else None
    begin_odd, end_odd = 0 if head else begin - REACH, tiles if tail else end - REACH
    odd_parts = [i for i in range(count) if MAIN in doing and cuts[i] < end_odd and cuts[i + 1] > begin_odd]
    own_parts = [i for i in range(count) if emit and cuts[i] < out[1] and cuts[i + 1] > out[0]]
    fixed = [*(own[i] for i in own_parts), *(odd[i] for i in odd_parts), *edges]
    first = 2 + len(fixed) + len(arrived)

    def kernel(own_list, odd_list, *refs):
        *refs, table, odd_table, listed = refs
        own_refs = dict(zip(own_parts, refs))
        odd_refs = dict(zip(odd_parts, refs[len(own_parts) :]))
        edge_refs = refs[len(own_parts) + len(odd_parts) : len(fixed)]
        came = refs[len(fixed) : first - 2]
        kept, wide, *outs = refs[first - 2 + len(keeps) :]
        kind = kind_here()
        place, odd_place = places(table, tiles), places(odd_table, tiles)

        @pl.when(kind == 2 * step)
        def _():
            lists = []
            if MAIN in doing:
                lists = [pltpu.make_async_copy(own_list, table, listed.at[0]), pltpu.make_async_copy(odd_list, odd_table, listed.at[1])]
            for copy in lists:
                copy.start()
            if step > 0 and FILL in doing:
                wide[rows_of(WIDE + begin, end - begin), :] = came[0][...]
            for m in range(WIDE * (FILL in doing)):
                if head:
                    value = came[1][rows_of(m), :] if step > 0 else edge_refs[0][rows_of(REACH), m * bond : (m + 1) * bond]
                    wide[rows_of(WIDE - 1 - m), :] = value
                if tail:
                    value = came[-1][rows_of(m), :] if step > 0 else edge_refs[-1][rows_of(REACH), m * bond : (m + 1) * bond]
                    wide[rows_of(tiles + 2 * WIDE - 1 - m), :] = value
            for e in range(REACH * (EDGE in doing)):
                if head:
                    kept[rows_of(REACH - 1 - e), :] = product(edge_refs[0][rows_of(e), :], wide[rows_of(WIDE - 1 - e - REACH, BAND), :])
                if tail:
                    at = tiles + REACH - 1 - e
                    kept[rows_of(REACH + at), :] = product(edge_refs[-1][rows_of(e), :], wide[rows_of(WIDE + at - REACH, BAND), :])
            for copy in lists:
                copy.wait()
            for p in range(begin_odd, end_odd if MAIN in doing else begin_odd):
                kept[rows_of(REACH + p), :] = product(blocks_at(odd_refs, cuts, p), stacked(wide, odd_place, p, WIDE, pairs))
            for p in range(*(out or (0, 0))):
                fresh = product(blocks_at(own_refs, cuts, p), stacked(kept, place, p, REACH, pairs))
                outs[0][rows_of(p - out[0]), :] = fresh
                if p < WIDE:
                    outs[1][rows_of(p), :] = fresh
                if p >= tiles - WIDE:
                    outs[-1][rows_of(p - (tiles - WIDE)), :] = fresh

        if give:

            @pl.when(kind % 2 == 0)
            def _():
                for (low, high), out in zip(give, outs[len(outs) - len(give) :]):
                    out[...] = wide[rows_of(WIDE + low, high - low), :]

    outs = [tile_rows(tiles + 2 * REACH, bond), tile_rows(tiles + 2 * WIDE, bond)]
    if emit:
        outs += [tile_rows(out[1] - out[0], bond)] + [tile_rows(WIDE, bond)] * (head + tail)
    outs += [tile_rows(high - low, bond) for low, high in give]
    return pl.pallas_call(
        kernel,
        in_specs=[ANY] * 2 + [VMEM] * (first - 2 + len(keeps)),
        out_specs=[VMEM] * len(outs),
        out_shape=outs,
        input_output_aliases={first + i: 2 - len(keeps) + i for i in range(len(keeps))},
        scratch_shapes=[pltpu.SMEM(tables[0].shape, jnp.int32)] * 2 + [pltpu.SemaphoreType.DMA((2,))],
        compiler_params=params(),
        cost_estimate=cost(work or STEP * (end - begin) / tiles),
        name="pair_step",
    )(*tables, *fixed, *arrived, *keeps)


def finish(begin, end, odd_column, tiles, pairs, cuts, table, own, given, regions, left, state, done, extra=()):
    bond = state.shape[1]
    parts = [k for k in range(len(own)) if cuts[k] < end and cuts[k + 1] > begin]
    limit = max(begin, end - GROUP)
    groups = [(p, min(GROUP, limit - p)) for p in range(begin, limit, GROUP)] + [(p, 1) for p in range(limit, end)]
    refs_in = [*(own[k] for k in parts), *given, *extra, left, state, *done]
    count, fixed = len(parts), len(parts) + len(given) + len(extra) + 2

    def kernel(own_list, *refs):
        own_refs = dict(zip(parts, refs))
        *taken, rows = refs[count : fixed - 1]
        kept, env, grad, staged_env, staged, sent, table, listed = refs[len(refs_in) :]

        core = kind_here() % 2
        lists = pltpu.make_async_copy(own_list, table, listed)

        @pl.when(core == 1)
        def _():
            for (low, high), value in zip(regions, taken):
                kept[rows_of(REACH + low, high - low), :] = value[...]

        @pl.when(core >= 0 if odd_column is None else core == odd_column)
        def _():
            lists.start()
            lists.wait()
            place = places(table, tiles)
            back = reversed_here()
            copies = []
            for g, (p, size) in enumerate(groups):
                start = jnp.where(back, tiles - p - size, p)
                for i in range(size):
                    inside = jnp.where(back, size - 1 - i, i)
                    sources = stacked(kept, place, p + i, REACH, pairs)
                    staged_env[rows_of(p - begin + inside), :] = product(blocks_at(own_refs, cuts, p + i), sources)
                    block = lax.dot_general(
                        rows[rows_of(start + inside), :], sources, (((1,), (1,)), ((), ())), preferred_element_type=jnp.float32
                    ).astype(jnp.bfloat16)
                    block = jnp.stack([block[:, j * TILE : (j + 1) * TILE] for j in range(pairs)], axis=0)
                    staged[rows_of(p - begin + inside)] = jnp.swapaxes(block, 0, 1)
                here, there = rows_of(p - begin, size), rows_of(start, size)
                copies.append(pltpu.make_async_copy(staged_env.at[here], env.at[there], sent.at[0, g]))
                copies.append(pltpu.make_async_copy(staged.at[here], grad.at[there], sent.at[1, g]))
                for copy in copies[-2:]:
                    copy.start()
            for copy in copies:
                copy.wait()

    env = tile_rows(tiles, bond)
    grad = jax.ShapeDtypeStruct((tiles * TILE, pairs, TILE), jnp.bfloat16)
    size = (end - begin) * TILE
    return pl.pallas_call(
        kernel,
        in_specs=[ANY] + [VMEM] * fixed + [HBM] * len(done),
        out_specs=[VMEM, HBM, HBM],
        out_shape=[tile_rows(tiles + 2 * REACH, bond), env, grad],
        input_output_aliases={fixed + i: i for i in range(1 + len(done))},
        scratch_shapes=[
            pltpu.VMEM((size, bond), jnp.bfloat16),
            pltpu.VMEM((size, pairs, TILE), jnp.bfloat16),
            pltpu.SemaphoreType.DMA((2, len(groups))),
            pltpu.SMEM(table.shape, jnp.int32),
            pltpu.SemaphoreType.DMA,
        ],
        compiler_params=params(),
        cost_estimate=cost(FINISH if odd_column == 0 else FINISH * (end - begin) / tiles),
        name="finish",
    )(table, *refs_in)


def limits(tiles, crossings):
    room = WIDE * crossings
    ends = [e for e in (13 * tiles // 32, 25 * tiles // 32) if room <= e <= tiles - WIDE]
    return ends or [tiles - WIDE]


def per_device(env_right, transfer, sources, env_left):
    ncol, nsec = lax.axis_size("col"), lax.axis_size("sec")
    layers = ncol // 2
    blocks = transfer[0, 0]
    length, pairs = blocks.shape[0], blocks.shape[1]
    tiles = length // TILE
    right, left = env_right[0], env_left[0, 0]

    def move(value, hops):
        both = [(a * nsec + s, b * nsec + to(s)) for a, b, to in hops for s in range(nsec) if 0 <= to(s) < nsec]
        return lax.ppermute(value, ("col", "sec"), both)

    def same(s):
        return s

    swap = [(c, c ^ 1, same) for c in range(ncol)]

    table = sources[0, 0].T

    ends = limits(tiles, layers - 1)
    count = len(ends) + 1
    cuts = [0] + [e + WIDE - REACH for e in ends] + [tiles]
    first_edge, last_edge = prepare_edges(pairs, tiles, table, blocks, right)
    first_edge, last_edge, blocks = lax.optimization_barrier((first_edge, last_edge, blocks))
    head, wide = prepare(0, 1, cuts, pairs, blocks, right)
    middle = prepare(1, count - 1, cuts, pairs, blocks, right) if count > 2 else []
    own = [head, *middle]
    odd_cols = [(2 * z + 1, 2 * z) for z in range(layers)]
    odd = [move(part, swap) for part in own]
    listed, _ = lax.optimization_barrier((table, head))
    odd_table = move(listed, swap)
    last_edge, _ = lax.optimization_barrier((last_edge, own[-1]))
    odd_edges = [move(first_edge, [(a, b, partner) for a, b in odd_cols]), move(last_edge, [(a, b, other) for a, b in odd_cols])]

    keeps = [wide]
    sent = None
    for step in range(layers):
        end = step == layers - 1
        inner = [0] + [e - WIDE * (step - 1) for e in ends] + [tiles]
        outer = None if end else [0] + [e - WIDE * step for e in ends] + [tiles]
        above, here = 2 * (layers - step), 2 * (layers - 1 - step)
        leaving = []
        for k in range(count):
            came = []
            if step > 0:
                came = [move(sent[k][0], [(above, here, same)])]
                if k == 0:
                    came.append(move(sent[k][1], [(above, here, partner)]))
                if k == count - 1:
                    came.append(halo if end else move(sent[k][-1], [(above, here, other)]))
                if end and k == count - 2:
                    halo = move(sent[k + 1][-1], [(above, here, other)])
            give = []
            if end and k == count - 2:
                middle = inner[k + 1] // 2
                give = [(-REACH, middle), (middle, inner[k + 1])]
            if end and k == count - 1:
                give = [(inner[k], tiles + REACH)]
            arguments = [table, odd_table], own, odd, odd_edges, came
            if step == 0 and k == 0:
                keeps = pair_step(step, k, tiles, pairs, cuts, inner, None, *arguments, keeps, (), (FILL, EDGE), FIRST)
                result = pair_step(step, k, tiles, pairs, cuts, inner, outer, *arguments, keeps, (), (MAIN,))
                own += prepare(count - 1, count, cuts, pairs, lax.optimization_barrier((blocks, result[2]))[0], right)
                odd.append(move(own[-1], swap))
            elif end and k == count - 1:
                *keeps, gift = pair_step(step, k, tiles, pairs, cuts, inner, None, *arguments, keeps, give, (FILL,), COLLECT)
                result = pair_step(step, k, tiles, pairs, cuts, inner, None, *arguments, keeps, (), (EDGE, MAIN))
            else:
                result = pair_step(step, k, tiles, pairs, cuts, inner, outer, *arguments, keeps, give, work=SECOND * (step == 0 and k == 1))
            keeps = list(result[:2])
            if give:
                gifts = [gift] if k == count - 1 else result[len(result) - len(give) :]
                given = [move(value, swap) for value in gifts]
                if k == count - 2:
                    half = max(0, give[-1][1] - WIDE) // GROUP * GROUP
                    done = []
                    for odd_column in (0, 1):
                        takes = (given, give) if odd_column else ([], [])
                        extra = [] if odd_column else [halo]
                        keeps[0], *done = finish(0, half, odd_column, tiles, pairs, cuts, table, own, *takes, left, keeps[0], done, extra)
                else:
                    _, env, grad = finish(half, tiles, None, tiles, pairs, cuts, table, own, given, give, left, keeps[0], done)
            leaving.append(result[2:])
        sent = leaving

    return env[None, None], grad[None, None]


def solution(mesh):
    placed = (
        P(None, "sec", None),
        P("col", None, "sec", None, None),
        P("col", None, "sec", None),
        P("col", None, "sec", None),
    )
    return jax.shard_map(
        per_device,
        mesh=mesh,
        in_specs=placed,
        out_specs=(P("col", None, "sec", None), P("col", None, "sec", None, None)),
        check_vma=False,
    )
```

```python
import jax
import jax.numpy as jnp
from jax import lax
from jax.experimental import pallas as pl
from jax.experimental.pallas import tpu as pltpu
from jax.sharding import PartitionSpec as P

TILE = 128
REACH = 2
WIDE = 2 * REACH
BAND = 2 * REACH + 1
GROUP = 4
FILL, EDGE, MAIN = range(3)
PREPARE, FIRST, SECOND, STEP, COLLECT, FINISH = 1e9, 2e10, 2e10, 1e10, 1e9, 4e9
VMEM = pl.BlockSpec(memory_space=pltpu.VMEM)
HBM = pl.BlockSpec(memory_space=pltpu.HBM)
ANY = pl.BlockSpec(memory_space=pl.ANY)


def params():
    return pltpu.CompilerParams(vmem_limit_bytes=16 * 1024 * 1024)


def cost(flops):
    return pl.CostEstimate(flops=int(flops), bytes_accessed=0, transcendentals=0)


def rows_of(tile, count=1):
    start = tile * TILE
    if not isinstance(start, int):
        start = pl.multiple_of(start, TILE)
    return pl.ds(start, count * TILE)


def tile_rows(count, width):
    return jax.ShapeDtypeStruct((count * TILE, width), jnp.bfloat16)


def kind_here():
    ncol, col = lax.axis_size("col"), lax.axis_index("col")
    return 2 * (ncol // 2 - 1 - col // 2) + col % 2


def reversed_here():
    return lax.axis_index("sec") % 2 == 0


def partner(s):
    return s + 1 if s % 2 == 0 else s - 1


def other(s):
    return s - 1 if s % 2 == 0 else s + 1


def places(table, tiles):
    back = reversed_here()
    base = lax.axis_index("sec") * tiles
    sign, flip = jnp.where(back, -1, 1), jnp.where(back, tiles - 1, 0)
    origin = jnp.where(back, tiles - 1 + base, -base)
    return lambda j, p: sign * table[j, sign * p + flip] + origin


def stacked(state, place, p, shift, pairs):
    return jnp.concatenate([state[rows_of(place(j, p) + shift), :] for j in range(pairs)], axis=0)


def product(blocks, state):
    return jnp.dot(blocks, state, preferred_element_type=jnp.float32).astype(jnp.bfloat16)


def blocks_at(parts, cuts, p):
    k = max(k for k in range(len(cuts) - 1) if cuts[k] <= p)
    return parts[k][rows_of(p - cuts[k]), :]


def prepare_edges(pairs, tiles, table, transfer, right):
    bond = right.shape[1]
    starts = [0, tiles - WIDE]

    def kernel(sources, source, environment, first, last, landed, halo, table, arrived, listed):
        back = reversed_here()
        place = places(table, tiles)
        copies = []
        for e, (near, begin) in enumerate(((0, 0), (tiles - REACH, starts[1]))):
            start = jnp.where(back, tiles - REACH - near, near)
            copies.append(pltpu.make_async_copy(source.at[rows_of(start, REACH)], landed.at[rows_of(e * REACH, REACH)], arrived.at[0, e]))
            start = jnp.where(back, tiles - WIDE - begin, begin)
            copies.append(pltpu.make_async_copy(environment.at[rows_of(start, WIDE)], halo.at[rows_of(e * WIDE, WIDE)], arrived.at[1, e]))
        lists = pltpu.make_async_copy(sources, table, listed)
        for copy in [lists, *copies]:
            copy.start()
        first[...] = jnp.zeros_like(first)
        last[...] = jnp.zeros_like(last)
        lists.wait()
        for e, (edge, near) in enumerate(((first, 0), (last, tiles - REACH))):
            copies[2 * e].wait()
            for i in range(REACH):
                p = near + i
                split = jnp.swapaxes(landed[rows_of(e * REACH + jnp.where(back, REACH - 1 - i, i))], 0, 1)
                for j in range(pairs):
                    edge[rows_of(i), rows_of(REACH - place(j, p) + p)] = split[j]
            copies[2 * e + 1].wait()
            for m in range(WIDE):
                at = e * WIDE + jnp.where(back, WIDE - 1 - m, m)
                edge[rows_of(REACH), m * bond : (m + 1) * bond] = halo[rows_of(at), :]

    return pl.pallas_call(
        kernel,
        in_specs=[HBM, HBM, HBM],
        out_specs=[VMEM, VMEM],
        out_shape=[tile_rows(REACH + 1, BAND * TILE)] * 2,
        scratch_shapes=[
            pltpu.VMEM((2 * REACH * TILE, pairs, TILE), jnp.bfloat16),
            pltpu.VMEM((2 * WIDE * TILE, bond), jnp.bfloat16),
            pltpu.SMEM(table.shape, jnp.int32),
            pltpu.SemaphoreType.DMA((2, 2)),
            pltpu.SemaphoreType.DMA,
        ],
        compiler_params=params(),
        cost_estimate=cost(PREPARE / 8),
        name="prepare_edges",
    )(*(pltpu.with_memory_space_constraint(value, pltpu.HBM) for value in (table, transfer, right)))


def prepare(first, final, cuts, pairs, transfer, right):
    tiles, bond = cuts[-1], right.shape[1]
    chosen = range(first, final)
    groups = [(p, min(GROUP, cuts[k + 1] - p)) for k in chosen for p in range(cuts[k], cuts[k + 1], GROUP)]
    begin, end = cuts[first], cuts[final]
    with_environment = first == 0

    def kernel(source, environment, *refs):
        parts, refs = refs[: len(chosen)], refs[len(chosen) :]
        landed, arrived, placed = refs[-3:]
        back = reversed_here()
        copies, whole = [], []
        for g, (p, size) in enumerate(groups):
            start = jnp.where(back, tiles - p - size, p)
            copies.append(pltpu.make_async_copy(source.at[rows_of(start, size)], landed.at[rows_of(p - begin, size)], arrived.at[g]))
        if with_environment:
            for p in range(tiles):
                at = jnp.where(back, tiles - 1 - p, p)
                whole.append(pltpu.make_async_copy(environment.at[rows_of(at)], refs[0].at[rows_of(WIDE + p)], placed.at[p]))
        for copy in copies + whole:
            copy.start()
        for g, (p, size) in enumerate(groups):
            copies[g].wait()
            k = max(k for k in chosen if cuts[k] <= p)
            for i in range(size):
                at = p - begin + jnp.where(back, size - 1 - i, i)
                split = jnp.swapaxes(landed[rows_of(at)], 0, 1)
                for j in range(pairs):
                    parts[k - first][rows_of(p + i - cuts[k]), j * TILE : (j + 1) * TILE] = split[j]
        for copy in whole:
            copy.wait()

    outs = [tile_rows(cuts[k + 1] - cuts[k], pairs * TILE) for k in chosen]
    if with_environment:
        outs.append(tile_rows(tiles + 2 * WIDE, bond))
    return pl.pallas_call(
        kernel,
        in_specs=[HBM, HBM],
        out_specs=[VMEM] * len(outs),
        out_shape=outs,
        scratch_shapes=[
            pltpu.VMEM(((end - begin) * TILE, pairs, TILE), jnp.bfloat16),
            pltpu.SemaphoreType.DMA((len(groups),)),
            pltpu.SemaphoreType.DMA((tiles,)),
        ],
        compiler_params=params(),
        cost_estimate=cost(PREPARE * (end - begin) / tiles),
        name="prepare",
    )(*(pltpu.with_memory_space_constraint(value, pltpu.HBM) for value in (transfer, right)))


def pair_step(step, k, tiles, pairs, cuts, inner, outer, tables, own, odd, edges, arrived, keeps, give=(), doing=(FILL, EDGE, MAIN), work=0):
    count = len(cuts) - 1
    head, tail = k == 0, k == count - 1
    edges = (edges[:1] * head + edges[1:] * tail) * (EDGE in doing or step == 0 and FILL in doing)
    arrived = arrived * (FILL in doing)
    bond = keeps[-1].shape[1]
    begin, end = inner[k], inner[k + 1]
    emit = outer is not None and MAIN in doing
    out = (outer[k], outer[k + 1]) if emit else None
    begin_odd, end_odd = 0 if head else begin - REACH, tiles if tail else end - REACH
    odd_parts = [i for i in range(count) if MAIN in doing and cuts[i] < end_odd and cuts[i + 1] > begin_odd]
    own_parts = [i for i in range(count) if emit and cuts[i] < out[1] and cuts[i + 1] > out[0]]
    fixed = [*(own[i] for i in own_parts), *(odd[i] for i in odd_parts), *edges]
    first = 2 + len(fixed) + len(arrived)

    def kernel(own_list, odd_list, *refs):
        *refs, table, odd_table, listed = refs
        own_refs = dict(zip(own_parts, refs))
        odd_refs = dict(zip(odd_parts, refs[len(own_parts) :]))
        edge_refs = refs[len(own_parts) + len(odd_parts) : len(fixed)]
        came = refs[len(fixed) : first - 2]
        kept, wide, *outs = refs[first - 2 + len(keeps) :]
        kind = kind_here()
        place, odd_place = places(table, tiles), places(odd_table, tiles)

        @pl.when(kind == 2 * step)
        def _():
            lists = []
            if MAIN in doing:
                lists = [pltpu.make_async_copy(own_list, table, listed.at[0]), pltpu.make_async_copy(odd_list, odd_table, listed.at[1])]
            for copy in lists:
                copy.start()
            if step > 0 and FILL in doing:
                wide[rows_of(WIDE + begin, end - begin), :] = came[0][...]
            for m in range(WIDE * (FILL in doing)):
                if head:
                    value = came[1][rows_of(m), :] if step > 0 else edge_refs[0][rows_of(REACH), m * bond : (m + 1) * bond]
                    wide[rows_of(WIDE - 1 - m), :] = value
                if tail:
                    value = came[-1][rows_of(m), :] if step > 0 else edge_refs[-1][rows_of(REACH), m * bond : (m + 1) * bond]
                    wide[rows_of(tiles + 2 * WIDE - 1 - m), :] = value
            for e in range(REACH * (EDGE in doing)):
                if head:
                    kept[rows_of(REACH - 1 - e), :] = product(edge_refs[0][rows_of(e), :], wide[rows_of(WIDE - 1 - e - REACH, BAND), :])
                if tail:
                    at = tiles + REACH - 1 - e
                    kept[rows_of(REACH + at), :] = product(edge_refs[-1][rows_of(e), :], wide[rows_of(WIDE + at - REACH, BAND), :])
            for copy in lists:
                copy.wait()
            for p in range(begin_odd, end_odd if MAIN in doing else begin_odd):
                kept[rows_of(REACH + p), :] = product(blocks_at(odd_refs, cuts, p), stacked(wide, odd_place, p, WIDE, pairs))
            for p in range(*(out or (0, 0))):
                fresh = product(blocks_at(own_refs, cuts, p), stacked(kept, place, p, REACH, pairs))
                outs[0][rows_of(p - out[0]), :] = fresh
                if p < WIDE:
                    outs[1][rows_of(p), :] = fresh
                if p >= tiles - WIDE:
                    outs[-1][rows_of(p - (tiles - WIDE)), :] = fresh

        if give:

            @pl.when(kind % 2 == 0)
            def _():
                for (low, high), out in zip(give, outs[len(outs) - len(give) :]):
                    out[...] = wide[rows_of(WIDE + low, high - low), :]

    outs = [tile_rows(tiles + 2 * REACH, bond), tile_rows(tiles + 2 * WIDE, bond)]
    if emit:
        outs += [tile_rows(out[1] - out[0], bond)] + [tile_rows(WIDE, bond)] * (head + tail)
    outs += [tile_rows(high - low, bond) for low, high in give]
    return pl.pallas_call(
        kernel,
        in_specs=[ANY] * 2 + [VMEM] * (first - 2 + len(keeps)),
        out_specs=[VMEM] * len(outs),
        out_shape=outs,
        input_output_aliases={first + i: 2 - len(keeps) + i for i in range(len(keeps))},
        scratch_shapes=[pltpu.SMEM(tables[0].shape, jnp.int32)] * 2 + [pltpu.SemaphoreType.DMA((2,))],
        compiler_params=params(),
        cost_estimate=cost(work or STEP * (end - begin) / tiles),
        name="pair_step",
    )(*tables, *fixed, *arrived, *keeps)


def finish(begin, end, odd_column, tiles, pairs, cuts, table, own, given, regions, left, state, done, extra=()):
    bond = state.shape[1]
    parts = [k for k in range(len(own)) if cuts[k] < end and cuts[k + 1] > begin]
    limit = max(begin, end - GROUP)
    groups = [(p, min(GROUP, limit - p)) for p in range(begin, limit, GROUP)] + [(p, 1) for p in range(limit, end)]
    refs_in = [*(own[k] for k in parts), *given, *extra, left, state, *done]
    count, fixed = len(parts), len(parts) + len(given) + len(extra) + 2

    def kernel(own_list, *refs):
        own_refs = dict(zip(parts, refs))
        *taken, rows = refs[count : fixed - 1]
        kept, env, grad, staged_env, staged, sent, table, listed = refs[len(refs_in) :]

        core = kind_here() % 2
        lists = pltpu.make_async_copy(own_list, table, listed)

        @pl.when(core == 1)
        def _():
            for (low, high), value in zip(regions, taken):
                kept[rows_of(REACH + low, high - low), :] = value[...]

        @pl.when(core >= 0 if odd_column is None else core == odd_column)
        def _():
            lists.start()
            lists.wait()
            place = places(table, tiles)
            back = reversed_here()
            copies = []
            for g, (p, size) in enumerate(groups):
                start = jnp.where(back, tiles - p - size, p)
                for i in range(size):
                    inside = jnp.where(back, size - 1 - i, i)
                    sources = stacked(kept, place, p + i, REACH, pairs)
                    staged_env[rows_of(p - begin + inside), :] = product(blocks_at(own_refs, cuts, p + i), sources)
                    block = lax.dot_general(
                        rows[rows_of(start + inside), :], sources, (((1,), (1,)), ((), ())), preferred_element_type=jnp.float32
                    ).astype(jnp.bfloat16)
                    block = jnp.stack([block[:, j * TILE : (j + 1) * TILE] for j in range(pairs)], axis=0)
                    staged[rows_of(p - begin + inside)] = jnp.swapaxes(block, 0, 1)
                here, there = rows_of(p - begin, size), rows_of(start, size)
                copies.append(pltpu.make_async_copy(staged_env.at[here], env.at[there], sent.at[0, g]))
                copies.append(pltpu.make_async_copy(staged.at[here], grad.at[there], sent.at[1, g]))
                for copy in copies[-2:]:
                    copy.start()
            for copy in copies:
                copy.wait()

    env = tile_rows(tiles, bond)
    grad = jax.ShapeDtypeStruct((tiles * TILE, pairs, TILE), jnp.bfloat16)
    size = (end - begin) * TILE
    return pl.pallas_call(
        kernel,
        in_specs=[ANY] + [VMEM] * fixed + [HBM] * len(done),
        out_specs=[VMEM, HBM, HBM],
        out_shape=[tile_rows(tiles + 2 * REACH, bond), env, grad],
        input_output_aliases={fixed + i: i for i in range(1 + len(done))},
        scratch_shapes=[
            pltpu.VMEM((size, bond), jnp.bfloat16),
            pltpu.VMEM((size, pairs, TILE), jnp.bfloat16),
            pltpu.SemaphoreType.DMA((2, len(groups))),
            pltpu.SMEM(table.shape, jnp.int32),
            pltpu.SemaphoreType.DMA,
        ],
        compiler_params=params(),
        cost_estimate=cost(FINISH if odd_column == 0 else FINISH * (end - begin) / tiles),
        name="finish",
    )(table, *refs_in)


def limits(tiles, crossings):
    room = WIDE * crossings
    ends = [e for e in (13 * tiles // 32, 25 * tiles // 32) if room <= e <= tiles - WIDE]
    return ends or [tiles - WIDE]


def per_device(env_right, transfer, sources, env_left):
    ncol, nsec = lax.axis_size("col"), lax.axis_size("sec")
    layers = ncol // 2
    blocks = transfer[0, 0]
    length, pairs = blocks.shape[0], blocks.shape[1]
    tiles = length // TILE
    right, left = env_right[0], env_left[0, 0]

    def move(value, hops):
        both = [(a * nsec + s, b * nsec + to(s)) for a, b, to in hops for s in range(nsec) if 0 <= to(s) < nsec]
        return lax.ppermute(value, ("col", "sec"), both)

    def same(s):
        return s

    swap = [(c, c ^ 1, same) for c in range(ncol)]

    table = sources[0, 0].T

    ends = limits(tiles, layers - 1)
    count = len(ends) + 1
    cuts = [0] + [e + WIDE - REACH for e in ends] + [tiles]
    first_edge, last_edge = prepare_edges(pairs, tiles, table, blocks, right)
    first_edge, last_edge, blocks = lax.optimization_barrier((first_edge, last_edge, blocks))
    head, wide = prepare(0, 1, cuts, pairs, blocks, right)
    middle = prepare(1, count - 1, cuts, pairs, blocks, right) if count > 2 else []
    own = [head, *middle]
    odd_cols = [(2 * z + 1, 2 * z) for z in range(layers)]
    odd = [move(part, swap) for part in own]
    listed, _ = lax.optimization_barrier((table, head))
    odd_table = move(listed, swap)
    last_edge, _ = lax.optimization_barrier((last_edge, own[-1]))
    odd_edges = [move(first_edge, [(a, b, partner) for a, b in odd_cols]), move(last_edge, [(a, b, other) for a, b in odd_cols])]

    keeps = [wide]
    sent = None
    for step in range(layers):
        end = step == layers - 1
        inner = [0] + [e - WIDE * (step - 1) for e in ends] + [tiles]
        outer = None if end else [0] + [e - WIDE * step for e in ends] + [tiles]
        above, here = 2 * (layers - step), 2 * (layers - 1 - step)
        leaving = []
        for k in range(count):
            came = []
            if step > 0:
                came = [move(sent[k][0], [(above, here, same)])]
                if k == 0:
                    came.append(move(sent[k][1], [(above, here, partner)]))
                if k == count - 1:
                    came.append(halo if end else move(sent[k][-1], [(above, here, other)]))
                if end and k == count - 2:
                    halo = move(sent[k + 1][-1], [(above, here, other)])
            give = []
            if end and k == count - 2:
                middle = inner[k + 1] // 2
                give = [(-REACH, middle), (middle, inner[k + 1])]
            if end and k == count - 1:
                give = [(inner[k], tiles + REACH)]
            arguments = [table, odd_table], own, odd, odd_edges, came
            if step == 0 and k == 0:
                keeps = pair_step(step, k, tiles, pairs, cuts, inner, None, *arguments, keeps, (), (FILL, EDGE), FIRST)
                result = pair_step(step, k, tiles, pairs, cuts, inner, outer, *arguments, keeps, (), (MAIN,))
                own += prepare(count - 1, count, cuts, pairs, lax.optimization_barrier((blocks, result[2]))[0], right)
                odd.append(move(own[-1], swap))
            elif end and k == count - 1:
                *keeps, gift = pair_step(step, k, tiles, pairs, cuts, inner, None, *arguments, keeps, give, (FILL,), COLLECT)
                result = pair_step(step, k, tiles, pairs, cuts, inner, None, *arguments, keeps, (), (EDGE, MAIN))
            else:
                result = pair_step(step, k, tiles, pairs, cuts, inner, outer, *arguments, keeps, give, work=SECOND * (step == 0 and k == 1))
            keeps = list(result[:2])
            if give:
                gifts = [gift] if k == count - 1 else result[len(result) - len(give) :]
                given = [move(value, swap) for value in gifts]
                if k == count - 2:
                    halves = max(0, give[-1][1] - WIDE), max(0, give[-1][1] - REACH)
                    done = []
                    for odd_column in (0, 1):
                        takes = (given, give) if odd_column else ([], [])
                        extra = [] if odd_column else [halo]
                        keeps[0], *done = finish(0, halves[odd_column], odd_column, tiles, pairs, cuts, table, own, *takes, left, keeps[0], done, extra)
                else:
                    state = keeps[0]
                    for odd_column in (0, 1):
                        takes = (given, give) if odd_column else ([], [])
                        begin = halves[odd_column]
                        state, *done = finish(begin, tiles, odd_column, tiles, pairs, cuts, table, own, *takes, left, state, done)
                    env, grad = done
            leaving.append(result[2:])
        sent = leaving

    return env[None, None], grad[None, None]


def solution(mesh):
    placed = (
        P(None, "sec", None),
        P("col", None, "sec", None, None),
        P("col", None, "sec", None),
        P("col", None, "sec", None),
    )
    return jax.shard_map(
        per_device,
        mesh=mesh,
        in_specs=placed,
        out_specs=(P("col", None, "sec", None), P("col", None, "sec", None, None)),
        check_vma=False,
    )
```
